128 devices in a mesh: ty: 8 (over z, x_lo), tx: 16 (over x_hi, y, core).
Axes of the slice: x: 4 (x_hi: 2, x_lo: 2; x = x_hi * 2 + x_lo), y: 4, z: 4, core: 2. Of those that a mesh axis runs over, the one named last changes fastest.
Arguments:
- object_slices: float32 [2, 2, 2048, 4096], P(None, None, 'ty', 'tx'), may hold values from -4 to 4
- probe_rows: float32 [2048, 256], P(('ty', 'tx')), may hold values from -4 to 4
- measured: float32 [8, 16, 2, 256, 256], P('ty', None, None, 'tx'), may hold values from 0.2 to 1.6
- positions: int32 [8, 16, 2, 2], P('ty', 'tx'), may hold values from 0 to 255
- counts: int32 [8, 16], P('ty', 'tx'), may hold values from 1 to 2, as said below
Outputs:
- object_grad: float32 [2, 2, 2048, 4096], P(None, None, 'ty', 'tx')
- probe_grad: float32 [2048, 256], P(('ty', 'tx'))
The draws below stay inside these ranges and needn't reach their ends.
Inputs may be any that keep to these rules, and one draw needn't show every extreme that they name: Slots s with s >= counts of their tile are unused; at least one tile has all 2 slots live.
All inputs are finite; a program needn't handle non-finite values.
Results may differ from the reference program's by a relative error of at most 0.0003.
Values sent between devices are 32-bit elements; how exact they have to be, the bound alone decides.
No kernel may reach another device: no remote copies, remote signals or barrier semaphores. Data moves between devices by JAX's collectives and lax.ppermute only.
A program may use at most 128 MiB of HBM per device.

```python
import math
import jax
import jax.numpy as jnp
from jax import lax

W = 256
MODES = 4
NSL = 2
K = 2
TILE = 256
NY = 2048
NX = 4096
SLOTS = 256
N_TY = 8
N_TX = 16


def draw_counts(key, part):
    key = jax.random.fold_in(key, 3)
    key_counts, key_pick = jax.random.split(key)
    tile_total = N_TY * N_TX
    base_counts = jax.random.randint(key_counts, (tile_total,), 1, K + 1)
    pick_index = jax.random.randint(key_pick, (), 0, tile_total)
    base_counts = jnp.where(jnp.arange(tile_total) == pick_index, K, base_counts)
    return base_counts.reshape(N_TY, N_TX).astype(jnp.int32)


def place_ends(result, stream_key, low, top_value):
    spot = [jax.random.randint(jax.random.fold_in(stream_key, axis), (), 0, length) for axis, length in enumerate(result.shape)]
    main_axis = result.shape.index(max(result.shape))
    neighbour = spot[:main_axis] + [(spot[main_axis] + 1) % result.shape[main_axis]] + spot[main_axis + 1:]
    return result.at[tuple(spot)].set(low).at[tuple(neighbour)].set(top_value)


def steps_of(stream_key, shape, pieces, low, largest):
    loudness = 1.0
    for dim, blocks in pieces:
        steps = jax.random.uniform(jax.random.fold_in(jax.random.fold_in(stream_key, 6), dim), (blocks,), jnp.float32, low / len(pieces), largest / len(pieces))
        loudness = loudness * jnp.repeat(jnp.exp(steps), shape[dim] // blocks).reshape((-1,) + (1,) * (len(shape) - 1 - dim))
    return loudness


def normal_values(rng, dims, width, bound, shards=(), held_as=jnp.bfloat16):
    loudness = steps_of(rng, dims, shards, -0.22, 0.18) if shards else 1.0
    array = jax.random.normal(rng, dims, jnp.float32) * width * loudness
    return jnp.minimum(jnp.maximum(array, -bound), bound).astype(held_as)


def setup_inputs(seed: int = 0) -> dict:
    keys = jax.random.split(jax.random.key(seed), 6)
    object_slices = normal_values(keys[0], (NSL, 2, NY, NX), 0.7, 4.0, ((2, 8), (3, 16)), jnp.float32)
    probe_rows = normal_values(keys[1], (2 * MODES * W, W), 0.5, 4.0, ((0, 128),), jnp.float32)
    measured = jnp.clip(0.2 + 1.4 * jax.random.uniform(keys[2], (N_TY, N_TX, K, W, W), jnp.float32) ** steps_of(keys[2], (N_TY, N_TX, K, W, W), ((0, 8), (3, 16)), -0.2, 0.2), 0.2, 1.6)
    positions = place_ends(jax.random.randint(keys[3], (N_TY, N_TX, K, 2), 0, TILE), jax.random.fold_in(keys[3], 1), 0, TILE - 1).astype(jnp.int32)
    counts = draw_counts(jax.random.fold_in(keys[5], 71), 0)
    return {"object_slices": object_slices, "probe_rows": probe_rows, "measured": measured, "positions": positions, "counts": counts}


amp_floor = 0.5

def matmul_high(form, first, second):
    return jnp.einsum(form, first, second, precision=lax.Precision.HIGHEST)

def make_tables(pattern_side):
    indices = jnp.arange(pattern_side, dtype=jnp.int32)
    product = indices[:, None] * indices[None, :] % pattern_side
    angles = 2.0 * math.pi / pattern_side * product.astype(jnp.float32)
    norm_factor = 1.0 / math.sqrt(pattern_side)
    cos_table = jnp.cos(angles) * norm_factor
    sin_table = jnp.sin(angles) * norm_factor
    frequency = (indices + pattern_side // 2) % pattern_side - pattern_side // 2
    quad = (frequency[:, None] * frequency[:, None] + frequency[None, :] * frequency[None, :]) % (4 * pattern_side)
    phase = 2.0 * math.pi / (4 * pattern_side) * quad.astype(jnp.float32)
    return (cos_table, sin_table, jnp.cos(phase), jnp.sin(phase))

def transform(real_part, imag_part, cos_table, sin_table):
    left_real = matmul_high('kn,mnc->mkc', cos_table, real_part) - matmul_high('kn,mnc->mkc', sin_table, imag_part)
    left_imag = matmul_high('kn,mnc->mkc', cos_table, imag_part) + matmul_high('kn,mnc->mkc', sin_table, real_part)
    out_real = matmul_high('mkc,cl->mkl', left_real, cos_table) - matmul_high('mkc,cl->mkl', left_imag, sin_table)
    out_imag = matmul_high('mkc,cl->mkl', left_imag, cos_table) + matmul_high('mkc,cl->mkl', left_real, sin_table)
    return (out_real, out_imag)

def slot_loss(window, probe, amplitude, weight, tables):
    cos_table, sin_table, prop_real, prop_imag = tables
    real_part = probe[:, 0]
    imag_part = probe[:, 1]
    slice_count = window.shape[0]
    for which in range(slice_count):
        obj_real = window[which, 0]
        obj_imag = window[which, 1]
        real_part, imag_part = (real_part * obj_real - imag_part * obj_imag, real_part * obj_imag + imag_part * obj_real)
        if which + 1 < slice_count:
            real_part, imag_part = transform(real_part, imag_part, cos_table, -sin_table)
            real_part, imag_part = (real_part * prop_real - imag_part * prop_imag, real_part * prop_imag + imag_part * prop_real)
            real_part, imag_part = transform(real_part, imag_part, cos_table, sin_table)
    real_part, imag_part = transform(real_part, imag_part, cos_table, -sin_table)
    intensity = lax.optimization_barrier(jnp.sum(real_part * real_part + imag_part * imag_part, axis=0))
    residual = jnp.sqrt(intensity + amp_floor) - amplitude
    return weight * jnp.sum(residual * residual)

def slot_gradient(window, probe, amplitude, weight, tables):
    loss_value, pullback = jax.vjp(lambda wind, prob: slot_loss(wind, prob, amplitude, weight, tables), window, probe)
    return pullback(jnp.ones_like(loss_value))

def reference(object_slices, probe_rows, measured, positions, counts):
    rim_width = W // 2
    probe = probe_rows.reshape(MODES, 2, W, W)
    padded = jnp.pad(object_slices, ((0, 0), (0, 0), (rim_width, rim_width), (rim_width, rim_width)))
    spot_rows = positions.reshape(SLOTS, 2)
    patterns = measured.reshape(SLOTS, W, W)
    live_counts = counts.reshape(N_TY * N_TX)
    tables = make_tables(W)
    loss_scale = 1.0 / math.sqrt(SLOTS)
    zero_index = jnp.zeros((), jnp.int32)

    def step(state_pair, slot_index):
        grad_pad, grad_total = state_pair
        tile_index = slot_index // K
        row_dev = slot_index // (N_TX * K)
        col_dev = tile_index % N_TX
        row_start = (row_dev * TILE + spot_rows[slot_index, 0]).astype(jnp.int32)
        col_start = (col_dev * TILE + spot_rows[slot_index, 1]).astype(jnp.int32)
        corner = (zero_index, zero_index, row_start, col_start)
        window = lax.dynamic_slice(padded, corner, (NSL, 2, W, W))
        live_flag = (slot_index % K < live_counts[tile_index]).astype(jnp.float32)
        grad_window, grad_probe = slot_gradient(window, probe, patterns[slot_index], live_flag * loss_scale, tables)
        current = lax.dynamic_slice(grad_pad, corner, (NSL, 2, W, W))
        grad_pad = lax.dynamic_update_slice(grad_pad, current + grad_window, corner)
        return ((grad_pad, grad_total + grad_probe), None)
    start_pair = (jnp.zeros(padded.shape, jnp.float32), jnp.zeros(probe.shape, jnp.float32))
    final_pair, unused = lax.scan(step, start_pair, jnp.arange(SLOTS, dtype=jnp.int32))
    grad_pad, grad_total = final_pair
    object_grad = grad_pad[:, :, rim_width:rim_width + NY, rim_width:rim_width + NX]
    return (object_grad, grad_total.reshape(2 * MODES * W, W))
```

```python
import functools

import jax
import jax.numpy as jnp
import ml_dtypes
import numpy as np
from jax import lax
from jax.experimental import pallas as pl
from jax.experimental.pallas import tpu as pltpu
from jax.sharding import Mesh
from jax.sharding import PartitionSpec as P

W = 256
H = 128
MODES = 4
SLOTS = 2
amp_floor = 0.5
f32 = jnp.float32
bf16 = jnp.bfloat16
VMEM_BYTES = 50 << 20


def real_form(a):
    return np.block([[a.real, -a.imag], [a.imag, a.real]])


def make_tables():
    k = np.arange(W)
    dft_matrix = np.exp(-2j * np.pi * ((k[:, None] * k[None, :]) % W) / W) / np.sqrt(W)
    freq = (k + H) % W - H
    phase = np.exp(2j * np.pi * ((freq * freq) % (4 * W)) / (4 * W))
    circ = dft_matrix.conj() @ np.diag(phase) @ dft_matrix
    c0, c1 = circ[:H, :H], circ[H:, :H]
    mats = [(c0 + c1) / 2, (c0 - c1) / 2, dft_matrix[0::2, :H], dft_matrix[1::2, :H]]
    high, low = [], []
    for mat in mats:
        full = real_form(mat)
        for form in (full, full.T):
            top = form.astype(np.float32).astype(ml_dtypes.bfloat16)
            high.append(top)
            low.append((form - top.astype(np.float64)).astype(np.float32).astype(ml_dtypes.bfloat16))
    return np.stack(high), np.stack(low)


def split(x):
    top = x.astype(bf16)
    return top, (x - top.astype(f32)).astype(bf16)


dot = functools.partial(jnp.dot, preferred_element_type=f32)


def left_product(tabs, i, x):
    top, rest = split(x)
    hi, lo = tabs
    return dot(hi[i], top) + dot(lo[i], top) + dot(hi[i], rest)


def right_product(tabs, i, x):
    top, rest = split(x)
    hi, lo = tabs
    return dot(top, hi[i]) + dot(top, lo[i]) + dot(rest, hi[i])


def halves(x, axis):
    return (x[:H], x[H:]) if axis == 0 else (x[:, :H], x[:, H:])


def one_side(tabs, axis, ia, ib, xr, xi, fold_in, fold_out):
    (ar, br), (ai, bi) = halves(xr, axis), halves(xi, axis)
    if fold_in:
        ar, br, ai, bi = ar + br, ar - br, ai + bi, ai - bi
    product = left_product if axis == 0 else right_product
    ya = product(tabs, ia, jnp.concatenate([ar, ai], axis))
    yb = product(tabs, ib, jnp.concatenate([br, bi], axis))
    if fold_out:
        ya, yb = ya + yb, ya - yb
    (ar, ai), (br, bi) = halves(ya, axis), halves(yb, axis)
    return jnp.concatenate([ar, br], axis), jnp.concatenate([ai, bi], axis)


def propagate(tabs, xr, xi, adjoint):
    t = 1 if adjoint else 0
    xr, xi = one_side(tabs, 0, 0 + t, 2 + t, xr, xi, True, True)
    return one_side(tabs, 1, 1 - t, 3 - t, xr, xi, True, True)


def dft(tabs, xr, xi):
    xr, xi = one_side(tabs, 0, 4, 6, xr, xi, True, False)
    return one_side(tabs, 1, 5, 7, xr, xi, True, False)


def dft_adjoint(tabs, xr, xi):
    xr, xi = one_side(tabs, 0, 5, 7, xr, xi, False, True)
    return one_side(tabs, 1, 4, 6, xr, xi, False, True)


def params():
    return pltpu.CompilerParams(vmem_limit_bytes=VMEM_BYTES)


def struct(*shape):
    return jax.ShapeDtypeStruct(shape, f32)


def whole(*shape):
    return pl.BlockSpec(shape, lambda *_: (0,) * len(shape))


TABLE_SPECS = [whole(8, W, W), whole(8, W, W)]
SMEM = pl.BlockSpec(memory_space=pltpu.SMEM)
mode_block = pl.BlockSpec((1, 2, W, W), lambda m, s: (m, 0, 0, 0))
slot_block = pl.BlockSpec((1, 2, W, W), lambda m, s: (s, 0, 0, 0))
both_block = pl.BlockSpec((1, 1, 2, W, W), lambda m, s: (m, s, 0, 0, 0))
VMEM = pl.BlockSpec(memory_space=pltpu.VMEM)


def extract_kernel(pos, mid, top, bot, lft, rgt, cl, cr, win, ext):
    for p in range(2):
        ext[p, H : H + W, H : H + W] = mid[p]
        ext[p, 0:H, H : H + W] = top[p]
        ext[p, H + W :, H : H + W] = bot[p]
        ext[p, H : H + W, 0:H] = lft[p]
        ext[p, H : H + W, H + W :] = rgt[p]
        ext[p, 0:H, 0:H] = cl[0, p]
        ext[p, H + W :, 0:H] = cl[1, p]
        ext[p, 0:H, H + W :] = cr[0, p]
        ext[p, H + W :, H + W :] = cr[1, p]
    for s in range(SLOTS):
        r = pos[s, 0]
        c = pos[s, 1]
        rows = pl.ds(pl.multiple_of(r // 8 * 8, 8), W + 8)
        cols = pl.ds(pl.multiple_of(c // H * H, H), W + H)
        for p in range(2):
            part = pltpu.roll(ext[p, rows, cols], lax.rem(W + H - c % H, W + H), 1)[:, :W]
            win[s, p] = pltpu.roll(part, lax.rem(W + 8 - r % 8, W + 8), 0)[:W]


def extract(pos, mid, top, bot, lft, rgt, cl, cr):
    return pl.pallas_call(
        extract_kernel,
        in_specs=[SMEM] + [VMEM] * 7,
        out_specs=VMEM,
        out_shape=struct(SLOTS, 2, W, W),
        scratch_shapes=[pltpu.VMEM((2, 2 * W, 2 * W), f32)],
        compiler_params=params(),
    )(pos, mid, top, bot, lft, rgt, cl, cr)


def place_kernel(pos, grad, mid, top, bot, lft, rgt, cl, cr, ext):
    ext[...] = jnp.zeros_like(ext)
    for s in range(SLOTS):
        r = pos[s, 0]
        c = pos[s, 1]
        rows = pl.ds(pl.multiple_of(r // 8 * 8, 8), W + 8)
        cols = pl.ds(pl.multiple_of(c // H * H, H), W + H)
        for p in range(2):
            part = jnp.concatenate([grad[s, p], jnp.zeros((8, W), f32)], 0)
            part = pltpu.roll(part, r % 8, 0)
            part = jnp.concatenate([part, jnp.zeros((W + 8, H), f32)], 1)
            ext[p, rows, cols] += pltpu.roll(part, c % H, 1)
    for p in range(2):
        mid[p] = ext[p, H : H + W, H : H + W]
        top[p] = ext[p, 0:H, H : H + W]
        bot[p] = ext[p, H + W :, H : H + W]
        lft[p] = ext[p, H : H + W, 0:H]
        rgt[p] = ext[p, H : H + W, H + W :]
        cl[0, p] = ext[p, 0:H, 0:H]
        cl[1, p] = ext[p, H + W :, 0:H]
        cr[0, p] = ext[p, 0:H, H + W :]
        cr[1, p] = ext[p, H + W :, H + W :]


def place(pos, grad):
    return pl.pallas_call(
        place_kernel,
        in_specs=[SMEM, VMEM],
        out_specs=[VMEM] * 7,
        out_shape=[
            struct(2, W, W),
            struct(2, H, W),
            struct(2, H, W),
            struct(2, W, H),
            struct(2, W, H),
            struct(2, 2, H, H),
            struct(2, 2, H, H),
        ],
        scratch_shapes=[pltpu.VMEM((2, 2 * W, 2 * W), f32)],
        compiler_params=params(),
    )(pos, grad)


def first_kernel(hi, lo, probe, win, u):
    pr, pi = probe[0, 0], probe[0, 1]
    a, b = win[0, 0], win[0, 1]
    ur, ui = propagate((hi, lo), pr * a - pi * b, pr * b + pi * a, False)
    u[0, 0, 0] = ur
    u[0, 0, 1] = ui


def first(tabs, probe, win):
    return pl.pallas_call(
        first_kernel,
        grid=(probe.shape[0], SLOTS),
        in_specs=TABLE_SPECS + [mode_block, slot_block],
        out_specs=both_block,
        out_shape=struct(probe.shape[0], SLOTS, 2, W, W),
        compiler_params=params(),
    )(*tabs, probe, win)


def second_kernel(hi, lo, u, win, far, intensity):
    m, s = pl.program_id(0), pl.program_id(1)
    ur, ui = u[0, 0, 0], u[0, 0, 1]
    a, b = win[0, 0], win[0, 1]
    fr, fi = dft((hi, lo), ur * a - ui * b, ur * b + ui * a)
    far[0, 0, 0] = fr
    far[0, 0, 1] = fi
    power = fr * fr + fi * fi

    @pl.when(m == 0)
    def _():
        intensity[s] = power

    @pl.when(m != 0)
    def _():
        intensity[s] += power


def second(tabs, u, win):
    return pl.pallas_call(
        second_kernel,
        grid=(MODES, SLOTS),
        in_specs=TABLE_SPECS + [both_block, slot_block],
        out_specs=[both_block, whole(SLOTS, W, W)],
        out_shape=[struct(MODES, SLOTS, 2, W, W), struct(SLOTS, W, W)],
        compiler_params=params(),
    )(*tabs, u, win)


def scale_kernel(loss_scale, counts, perm, meas, intensity, scale):
    order = perm[...]
    for s in range(SLOTS):
        x = meas[:, s].reshape(W, W)
        pieces = []
        for _ in range(3):
            piece = x.astype(bf16)
            x = x - piece.astype(f32)
            pieces.append(piece)
        x = (dot(order, pieces[0]) + dot(order, pieces[1])) + dot(order, pieces[2])
        pieces = []
        for _ in range(3):
            piece = x.astype(bf16)
            x = x - piece.astype(f32)
            pieces.append(piece)
        turned = order.T
        x = (dot(pieces[0], turned) + dot(pieces[1], turned)) + dot(pieces[2], turned)
        weight = jnp.where(s < counts[0, 0], 2.0 * loss_scale, 0.0)
        scale[s] = weight * (1.0 - x * lax.rsqrt(intensity[s] + amp_floor))


def residual_scale(loss_scale, counts, meas, intensity):
    perm = np.zeros((W, W), ml_dtypes.bfloat16)
    perm[np.arange(W), np.concatenate([np.arange(0, W, 2), np.arange(1, W, 2)])] = 1
    return pl.pallas_call(
        functools.partial(scale_kernel, loss_scale),
        in_specs=[SMEM, VMEM, VMEM, VMEM],
        out_specs=VMEM,
        out_shape=struct(SLOTS, W, W),
        compiler_params=params(),
    )(counts, perm, meas, intensity)


def third_kernel(hi, lo, scale, far, u, win, grad_u, grad_win):
    m, s = pl.program_id(0), pl.program_id(1)
    factor = scale[0]
    gr, gi = dft_adjoint((hi, lo), factor * far[0, 0, 0], factor * far[0, 0, 1])
    ur, ui = u[0, 0, 0], u[0, 0, 1]
    a, b = win[0, 0], win[0, 1]
    grad_u[0, 0, 0] = gr * a + gi * b
    grad_u[0, 0, 1] = gi * a - gr * b
    wr = gr * ur + gi * ui
    wi = gi * ur - gr * ui

    @pl.when(m == 0)
    def _():
        grad_win[s, 0] = wr
        grad_win[s, 1] = wi

    @pl.when(m != 0)
    def _():
        grad_win[s, 0] += wr
        grad_win[s, 1] += wi


def third(tabs, scale, far, u, win):
    return pl.pallas_call(
        third_kernel,
        grid=(MODES, SLOTS),
        in_specs=TABLE_SPECS
        + [pl.BlockSpec((1, W, W), lambda m, s: (s, 0, 0)), both_block, both_block, slot_block],
        out_specs=[both_block, whole(SLOTS, 2, W, W)],
        out_shape=[struct(MODES, SLOTS, 2, W, W), struct(SLOTS, 2, W, W)],
        compiler_params=params(),
    )(*tabs, scale, far, u, win)


def fourth_kernel(hi, lo, grad_u, probe, win, grad_probe, grad_win):
    m, s = pl.program_id(0), pl.program_id(1)
    gr, gi = propagate((hi, lo), grad_u[0, 0, 0], grad_u[0, 0, 1], True)
    pr, pi = probe[0, 0], probe[0, 1]
    a, b = win[0, 0], win[0, 1]
    qr = gr * a + gi * b
    qi = gi * a - gr * b
    wr = gr * pr + gi * pi
    wi = gi * pr - gr * pi

    @pl.when(s == 0)
    def _():
        grad_probe[0, 0] = qr
        grad_probe[0, 1] = qi

    @pl.when(s != 0)
    def _():
        grad_probe[0, 0] += qr
        grad_probe[0, 1] += qi

    @pl.when(m == 0)
    def _():
        grad_win[s, 0] = wr
        grad_win[s, 1] = wi

    @pl.when(m != 0)
    def _():
        grad_win[s, 0] += wr
        grad_win[s, 1] += wi


def fourth(tabs, grad_u, probe, win):
    return pl.pallas_call(
        fourth_kernel,
        grid=(MODES, SLOTS),
        in_specs=TABLE_SPECS + [both_block, mode_block, slot_block],
        out_specs=[mode_block, whole(SLOTS, 2, W, W)],
        out_shape=[struct(MODES, 2, W, W), struct(SLOTS, 2, W, W)],
        compiler_params=params(),
    )(*tabs, grad_u, probe, win)


TY = ("z", "xl")
TX = ("xh", "y", "c")
PLANE = ("xl", "xh", "y")
SWAP = [(0, 1), (1, 0)]


def up_perm(count):
    return [(i, i + 1) for i in range(count - 1)]


def down_perm(count):
    return [(i + 1, i) for i in range(count - 1)]


def fold_rims(pieces):
    mid, top, bot, lft, rgt, cl, cr = pieces
    from_right = lax.ppermute(cl, TX, down_perm(16))
    from_left = lax.ppermute(cr, TX, up_perm(16))
    lft = lax.ppermute(lft, TX, down_perm(16))
    rgt = lax.ppermute(rgt, TX, up_perm(16))
    rims = jnp.stack([top, bot])
    rims = rims + jnp.concatenate([from_left, from_right], 3)
    below = lax.ppermute(rims[0], TY, down_perm(8))
    above = lax.ppermute(rims[1], TY, up_perm(8))
    return mid + jnp.concatenate([above, below], 1) + jnp.concatenate([rgt, lft], 2)


def body(object_slices, probe_rows, measured, positions, counts):
    tabs = tuple(jnp.asarray(t) for t in make_tables())
    pos = positions[0, 0]
    wins = []
    for j in range(2):
        mid = object_slices[j]
        top = lax.ppermute(mid[:, H:], TY, up_perm(8))
        bot = lax.ppermute(mid[:, :H], TY, down_perm(8))
        lft = lax.ppermute(mid[:, :, H:], TX, up_perm(16))
        rgt = lax.ppermute(mid[:, :, :H], TX, down_perm(16))
        rims = jnp.stack([top, bot])
        cl = lax.ppermute(rims[..., H:], TX, up_perm(16))
        cr = lax.ppermute(rims[..., :H], TX, down_perm(16))
        wins.append(extract(pos, mid, top, bot, lft, rgt, cl, cr))
    spread = jnp.broadcast_to(probe_rows[None], (32, 16, W))
    own = lax.all_to_all(spread, PLANE + ("c",), split_axis=0, concat_axis=0, tiled=True)
    own = own.reshape(2, W, W)
    chunks = [own] + [
        lax.ppermute(own, "z", [((i + j) % 4, i) for i in range(4)]) for j in range(1, 4)
    ]
    probe = jnp.stack(chunks)
    meas = lax.all_to_all(measured[0], TX, split_axis=0, concat_axis=0, tiled=True)
    u = first(tabs, probe, wins[0])
    far, intensity = second(tabs, u, wins[1])
    scale = residual_scale(1.0 / 16.0, counts, meas, intensity)
    grad_u, grad_win1 = third(tabs, scale, far, u, wins[1])
    folded1 = fold_rims(place(pos, grad_win1))
    grad_probe, grad_win0 = fourth(tabs, grad_u, probe, wins[0])
    folded0 = fold_rims(place(pos, grad_win0))
    core = lax.axis_index("c")
    cut = grad_probe.reshape(MODES, 16, 2, 16, W)
    mine = jnp.where(core == 0, cut[:, :, 0], cut[:, :, 1])
    other = jnp.where(core == 0, cut[:, :, 1], cut[:, :, 0])
    mine = mine + lax.ppermute(other, "c", SWAP)
    total = mine[0]
    for j in range(1, 4):
        total = total + lax.ppermute(mine[j], "z", [(i, (i + j) % 4) for i in range(4)])
    pieces = lax.all_to_all(total, PLANE, split_axis=0, concat_axis=0, tiled=True)
    return jnp.stack([folded0, folded1]), jnp.sum(pieces.reshape(16, 16, W), 0)


def solution(mesh):
    fine = Mesh(mesh.devices.reshape(4, 2, 2, 4, 2), ("z", "xl", "xh", "y", "c"))
    in_specs = (
        P(None, None, TY, TX),
        P(TY + TX, None),
        P(TY, None, None, TX, None),
        P(TY, TX, None, None),
        P(TY, TX),
    )
    out_specs = (P(None, None, TY, TX), P(TY + TX, None))
    return jax.shard_map(
        body, mesh=fine, in_specs=in_specs, out_specs=out_specs, check_vma=False
    )
```

```python
import functools

import jax
import jax.numpy as jnp
import ml_dtypes
import numpy as np
from jax import lax
from jax.experimental import pallas as pl
from jax.experimental.pallas import tpu as pltpu
from jax.sharding import Mesh
from jax.sharding import PartitionSpec as P

W = 256
H = 128
MODES = 4
SLOTS = 2
amp_floor = 0.5
f32 = jnp.float32
bf16 = jnp.bfloat16
VMEM_BYTES = 24 << 20


def real_form(a):
    return np.block([[a.real, -a.imag], [a.imag, a.real]])


def make_tables():
    k = np.arange(W)
    dft_matrix = np.exp(-2j * np.pi * ((k[:, None] * k[None, :]) % W) / W) / np.sqrt(W)
    freq = (k + H) % W - H
    phase = np.exp(2j * np.pi * ((freq * freq) % (4 * W)) / (4 * W))
    circ = dft_matrix.conj() @ np.diag(phase) @ dft_matrix
    c0, c1 = circ[:H, :H], circ[H:, :H]
    mats = [(c0 + c1) / 2, (c0 - c1) / 2, dft_matrix[0::2, :H], dft_matrix[1::2, :H]]
    high, low = [], []
    for mat in mats:
        full = real_form(mat)
        for form in (full, full.T):
            top = form.astype(np.float32).astype(ml_dtypes.bfloat16)
            high.append(top)
            low.append((form - top.astype(np.float64)).astype(np.float32).astype(ml_dtypes.bfloat16))
    return np.stack(high), np.stack(low)


def split(x):
    top = x.astype(bf16)
    return top, (x - top.astype(f32)).astype(bf16)


dot = functools.partial(jnp.dot, preferred_element_type=f32)


def left_product(tabs, i, x):
    top, rest = split(x)
    hi, lo = tabs
    return dot(hi[i], top) + dot(lo[i], top) + dot(hi[i], rest)


def right_product(tabs, i, x):
    top, rest = split(x)
    hi, lo = tabs
    return dot(top, hi[i]) + dot(top, lo[i]) + dot(rest, hi[i])


def halves(x, axis):
    return (x[:H], x[H:]) if axis == 0 else (x[:, :H], x[:, H:])


def one_side(tabs, axis, ia, ib, xr, xi, fold_in, fold_out):
    (ar, br), (ai, bi) = halves(xr, axis), halves(xi, axis)
    if fold_in:
        ar, br, ai, bi = ar + br, ar - br, ai + bi, ai - bi
    product = left_product if axis == 0 else right_product
    ya = product(tabs, ia, jnp.concatenate([ar, ai], axis))
    yb = product(tabs, ib, jnp.concatenate([br, bi], axis))
    if fold_out:
        ya, yb = ya + yb, ya - yb
    (ar, ai), (br, bi) = halves(ya, axis), halves(yb, axis)
    return jnp.concatenate([ar, br], axis), jnp.concatenate([ai, bi], axis)


def propagate(tabs, xr, xi, adjoint):
    t = 1 if adjoint else 0
    xr, xi = one_side(tabs, 0, 0 + t, 2 + t, xr, xi, True, True)
    return one_side(tabs, 1, 1 - t, 3 - t, xr, xi, True, True)


def dft(tabs, xr, xi):
    xr, xi = one_side(tabs, 0, 4, 6, xr, xi, True, False)
    return one_side(tabs, 1, 5, 7, xr, xi, True, False)


def dft_adjoint(tabs, xr, xi):
    xr, xi = one_side(tabs, 0, 5, 7, xr, xi, False, True)
    return one_side(tabs, 1, 4, 6, xr, xi, False, True)


def params():
    return pltpu.CompilerParams(vmem_limit_bytes=VMEM_BYTES)


def struct(*shape):
    return jax.ShapeDtypeStruct(shape, f32)


def whole(*shape):
    return pl.BlockSpec(shape, lambda *_: (0,) * len(shape))


TABLE_SPECS = [whole(8, W, W), whole(8, W, W)]
SMEM = pl.BlockSpec(memory_space=pltpu.SMEM)
mode_block = pl.BlockSpec((1, 2, W, W), lambda m, s: (m, 0, 0, 0))
slot_block = pl.BlockSpec((1, 2, W, W), lambda m, s: (s, 0, 0, 0))
both_block = pl.BlockSpec((1, 1, 2, W, W), lambda m, s: (m, s, 0, 0, 0))
VMEM = pl.BlockSpec(memory_space=pltpu.VMEM)


def cost(transforms):
    return pl.CostEstimate(flops=transforms * 1_200_000_000, bytes_accessed=1 << 20, transcendentals=0)


def row_slices_kernel(mid, up, down):
    up[...] = mid[:, :, H:, :]
    down[...] = mid[:, :, :H, :]


def row_slices(mid):
    block = pl.BlockSpec((1, 2, H, W), lambda j: (j, 0, 0, 0))
    return pl.pallas_call(
        row_slices_kernel,
        grid=(2,),
        in_specs=[pl.BlockSpec((1, 2, W, W), lambda j: (j, 0, 0, 0))],
        out_specs=[block, block],
        out_shape=[struct(2, 2, H, W)] * 2,
        compiler_params=params(),
    )(mid)


def column_slices_kernel(mid, top, bot, right, left):
    for out, cols in ((right, slice(H, W)), (left, slice(0, H))):
        out[:, :, 0:H] = top[:, :, :, cols]
        out[:, :, H : H + W] = mid[:, :, :, cols]
        out[:, :, H + W :] = bot[:, :, :, cols]


def column_slices(mid, top, bot):
    rim = pl.BlockSpec((1, 2, H, W), lambda j: (j, 0, 0, 0))
    tall = pl.BlockSpec((1, 2, 2 * W, H), lambda j: (j, 0, 0, 0))
    return pl.pallas_call(
        column_slices_kernel,
        grid=(2,),
        in_specs=[pl.BlockSpec((1, 2, W, W), lambda j: (j, 0, 0, 0)), rim, rim],
        out_specs=[tall, tall],
        out_shape=[struct(2, 2, 2 * W, H)] * 2,
        compiler_params=params(),
    )(mid, top, bot)


def corner(pos, s):
    r = pos[s, 0]
    c = pos[s, 1]
    rows = pl.ds(pl.multiple_of(r // 8 * 8, 8), W + 8)
    cols = [pl.ds(pl.multiple_of(c // H * H + k * H, H), H) for k in range(3)]
    return rows, cols, r % 8, c % H


def extract_kernel(pos, mid, top, bot, lft, rgt, win, ext):
    lane = lax.broadcasted_iota(jnp.int32, (W + 8, H), 1)
    sub = lax.broadcasted_iota(jnp.int32, (W // 8, 8, H), 1)
    for j in range(2):
        for p in range(2):
            ext[p, 0:H, H : H + W] = top[j, p]
            ext[p, H : H + W, H : H + W] = mid[j, p]
            ext[p, H + W :, H : H + W] = bot[j, p]
            ext[p, :, 0:H] = lft[j, p]
            ext[p, :, H + W :] = rgt[j, p]
        for s in range(SLOTS):
            rows, cols, dr, dc = corner(pos, s)
            for p in range(2):
                turned = [pltpu.roll(ext[p, rows, col], (H - dc) % H, 1) for col in cols]
                for k in range(2):
                    x = jnp.where(lane < H - dc, turned[k], turned[k + 1])
                    x = pltpu.roll(x.reshape(W // 8 + 1, 8, H), (8 - dr) % 8, 1)
                    x = jnp.where(sub < 8 - dr, x[:-1], x[1:])
                    win[s, j, p, :, k * H : k * H + H] = x.reshape(W, H)


def extract(pos, mid, top, bot, lft, rgt):
    return pl.pallas_call(
        extract_kernel,
        in_specs=[SMEM] + [VMEM] * 5,
        out_specs=VMEM,
        out_shape=struct(SLOTS, 2, 2, W, W),
        scratch_shapes=[pltpu.VMEM((2, 2 * W, 2 * W), f32)],
        compiler_params=params(),
        cost_estimate=cost(3),
    )(pos, mid, top, bot, lft, rgt)


def place_kernel(pos, grad, mid, top, bot, lft, rgt, ext):
    lane = lax.broadcasted_iota(jnp.int32, (W + 8, H), 1)
    sub = lax.broadcasted_iota(jnp.int32, (W // 8 + 1, 8, H), 1)
    group = jnp.zeros((1, 8, H), f32)
    for j in range(2):
        ext[...] = jnp.zeros_like(ext)
        for s in range(SLOTS):
            rows, cols, dr, dc = corner(pos, s)
            for p in range(2):
                turned = []
                for k in range(2):
                    x = grad[s, j, p, :, k * H : k * H + H].reshape(W // 8, 8, H)
                    x = pltpu.roll(x, dr, 1)
                    x = jnp.where(
                        sub >= dr,
                        jnp.concatenate([x, group], 0),
                        jnp.concatenate([group, x], 0),
                    )
                    turned.append(pltpu.roll(x.reshape(W + 8, H), dc, 1))
                ext[p, rows, cols[0]] += jnp.where(lane >= dc, turned[0], 0.0)
                ext[p, rows, cols[1]] += jnp.where(lane >= dc, turned[1], turned[0])
                ext[p, rows, cols[2]] += jnp.where(lane >= dc, 0.0, turned[1])
        for p in range(2):
            top[j, p] = ext[p, 0:H, H : H + W]
            mid[j, p] = ext[p, H : H + W, H : H + W]
            bot[j, p] = ext[p, H + W :, H : H + W]
            lft[j, p] = ext[p, :, 0:H]
            rgt[j, p] = ext[p, :, H + W :]


def place(pos, grad):
    return pl.pallas_call(
        place_kernel,
        in_specs=[SMEM, VMEM],
        out_specs=[VMEM] * 5,
        out_shape=[
            struct(2, 2, W, W),
            struct(2, 2, H, W),
            struct(2, 2, H, W),
            struct(2, 2, 2 * W, H),
            struct(2, 2, 2 * W, H),
        ],
        scratch_shapes=[pltpu.VMEM((2, 2 * W, 2 * W), f32)],
        compiler_params=params(),
        cost_estimate=cost(3),
    )(pos, grad)


def rims_kernel(top, bot, right, left, above, below, rows, sides, sems):
    pairs = [(top, rows.at[0]), (bot, rows.at[1])]
    for k, cells in ((0, pl.ds(0, H)), (1, pl.ds(H + W, H))):
        pairs.append((left.at[:, :, cells, :], sides.at[2 * k]))
        pairs.append((right.at[:, :, cells, :], sides.at[2 * k + 1]))
    copies = [pltpu.make_async_copy(a, b, sems.at[k]) for k, (a, b) in enumerate(pairs)]
    for copy in copies:
        copy.start()
    for copy in copies:
        copy.wait()
    for k, out in ((0, above), (1, below)):
        out[:, :, :, 0:H] = rows[k, :, :, :, 0:H] + sides[2 * k]
        out[:, :, :, H:] = rows[k, :, :, :, H:] + sides[2 * k + 1]


def rims(top, bot, from_right, from_left):
    return pl.pallas_call(
        rims_kernel,
        in_specs=[pl.BlockSpec(memory_space=pl.ANY)] * 4,
        out_specs=[VMEM] * 2,
        out_shape=[struct(2, 2, H, W)] * 2,
        scratch_shapes=[
            pltpu.VMEM((2, 2, 2, H, W), f32),
            pltpu.VMEM((4, 2, 2, H, H), f32),
            pltpu.SemaphoreType.DMA((6,)),
        ],
        compiler_params=params(),
    )(top, bot, from_right, from_left)


def combine_kernel(mid, right, left, above, below, out):
    near, far = slice(H, W), slice(W, W + H)
    out[:, :, 0:H, 0:H] = mid[:, :, 0:H, 0:H] + above[:, :, :, 0:H] + left[:, :, near]
    out[:, :, 0:H, H:] = mid[:, :, 0:H, H:] + above[:, :, :, H:] + right[:, :, near]
    out[:, :, H:, 0:H] = mid[:, :, H:, 0:H] + below[:, :, :, 0:H] + left[:, :, far]
    out[:, :, H:, H:] = mid[:, :, H:, H:] + below[:, :, :, H:] + right[:, :, far]


def combine(mid, from_right, from_left, above, below):
    return pl.pallas_call(
        combine_kernel,
        in_specs=[VMEM] * 5,
        out_specs=VMEM,
        out_shape=struct(2, 2, W, W),
        compiler_params=params(),
    )(mid, from_right, from_left, above, below)


probe_block = pl.BlockSpec((4, 1, 4, 16, W), lambda m, s: (0, m, 0, 0, 0))
grad_block = pl.BlockSpec((1, 4, 4, 16, W), lambda m, s: (m, 0, 0, 0, 0))
PROBE = (4, 4, 4, 16, W)


def block_rows(x, y, c):
    return pl.ds(pl.multiple_of((x % 2) * 128 + y * 32 + c * 16, 16), 16)


def join_probe(core, mine, other, probe):
    c = core[0]
    for x in range(4):
        for y in range(4):
            probe[x // 2, block_rows(x, y, c), :] = mine[y, 0, x]
            probe[x // 2, block_rows(x, y, 1 - c), :] = other[y, 0, x]


def cut_probe(core, probe, mine, other):
    c = core[0]
    for x in range(4):
        for y in range(4):
            mine[0, x, y] = probe[x // 2, block_rows(x, y, c), :]
            other[0, x, y] = probe[x // 2, block_rows(x, y, 1 - c), :]


def forward_kernel(core, hi, lo, mine, other, win, u, far, intensity, probe):
    m, s = pl.program_id(0), pl.program_id(1)

    @pl.when(s == 0)
    def _():
        join_probe(core, mine, other, probe)

    pr, pi = probe[0], probe[1]
    a, b = win[0, 0, 0], win[0, 0, 1]
    ur, ui = propagate((hi, lo), pr * a - pi * b, pr * b + pi * a, False)
    u[0, 0, 0] = ur
    u[0, 0, 1] = ui
    a, b = win[0, 1, 0], win[0, 1, 1]
    fr, fi = dft((hi, lo), ur * a - ui * b, ur * b + ui * a)
    far[0, 0, 0] = fr
    far[0, 0, 1] = fi
    power = fr * fr + fi * fi

    @pl.when(m == 0)
    def _():
        intensity[s] = power

    @pl.when(m != 0)
    def _():
        intensity[s] += power


window_block = pl.BlockSpec((1, 2, 2, W, W), lambda m, s: (s, 0, 0, 0, 0))


def forward(tabs, core, mine, other, win):
    return pl.pallas_call(
        forward_kernel,
        grid=(MODES, SLOTS),
        in_specs=[SMEM] + TABLE_SPECS + [probe_block, probe_block, window_block],
        out_specs=[both_block, both_block, whole(SLOTS, W, W)],
        scratch_shapes=[pltpu.VMEM((2, W, W), f32)],
        out_shape=[
            struct(MODES, SLOTS, 2, W, W),
            struct(MODES, SLOTS, 2, W, W),
            struct(SLOTS, W, W),
        ],
        compiler_params=params(),
        cost_estimate=cost(16),
    )(core, *tabs, mine, other, win)


def pieces_of(x):
    out = []
    for _ in range(3):
        out.append(x.astype(bf16))
        x = x - out[-1].astype(f32)
    return out


def even_odd_order():
    perm = np.zeros((W, W), ml_dtypes.bfloat16)
    perm[np.arange(W), np.concatenate([np.arange(0, W, 2), np.arange(1, W, 2)])] = 1
    return jnp.asarray(np.stack([perm, perm.T]))


def reordered(order, x):
    a, b, c = pieces_of(x)
    x = (dot(order[0], a) + dot(order[0], b)) + dot(order[0], c)
    a, b, c = pieces_of(x)
    return (dot(a, order[1]) + dot(b, order[1])) + dot(c, order[1])


def backward_kernel(
    loss_scale, core, counts, order, hi, lo, meas, intensity, far, u, mine, other, win,
    grad_mine, grad_other, grad_win, scale, probe, grad_probe,
):
    m, s = pl.program_id(0), pl.program_id(1)

    @pl.when(s == 0)
    def _():
        join_probe(core, mine, other, probe)

    @pl.when(m == 0)
    def _():
        weight = jnp.where(s < counts[0, 0], 2.0 * loss_scale, 0.0)
        amplitude = reordered(order, meas[:, 0].reshape(W, W))
        scale[s] = weight * (1.0 - amplitude * lax.rsqrt(intensity[0] + amp_floor))

    factor = scale[s]
    gr, gi = dft_adjoint((hi, lo), factor * far[0, 0, 0], factor * far[0, 0, 1])
    ur, ui = u[0, 0, 0], u[0, 0, 1]
    vr = gr * ur + gi * ui
    vi = gi * ur - gr * ui
    a, b = win[0, 1, 0], win[0, 1, 1]
    gr, gi = propagate((hi, lo), gr * a + gi * b, gi * a - gr * b, True)
    pr, pi = probe[0], probe[1]
    wr = gr * pr + gi * pi
    wi = gi * pr - gr * pi
    a, b = win[0, 0, 0], win[0, 0, 1]
    qr = gr * a + gi * b
    qi = gi * a - gr * b

    @pl.when(s == 0)
    def _():
        grad_probe[0] = qr
        grad_probe[1] = qi

    @pl.when(s != 0)
    def _():
        grad_probe[0] += qr
        grad_probe[1] += qi
        cut_probe(core, grad_probe, grad_mine, grad_other)

    @pl.when(m == 0)
    def _():
        grad_win[s, 0, 0] = wr
        grad_win[s, 0, 1] = wi
        grad_win[s, 1, 0] = vr
        grad_win[s, 1, 1] = vi

    @pl.when(m != 0)
    def _():
        grad_win[s, 0, 0] += wr
        grad_win[s, 0, 1] += wi
        grad_win[s, 1, 0] += vr
        grad_win[s, 1, 1] += vi


def backward(tabs, loss_scale, core, counts, meas, intensity, far, u, mine, other, win):
    return pl.pallas_call(
        functools.partial(backward_kernel, loss_scale),
        grid=(MODES, SLOTS),
        in_specs=[SMEM, SMEM, whole(2, W, W)]
        + TABLE_SPECS
        + [
            pl.BlockSpec((16, 1, 16, W), lambda m, s: (0, jnp.where(m == 0, s, 1), 0, 0)),
            pl.BlockSpec((1, W, W), lambda m, s: (jnp.where(m == 0, s, 1), 0, 0)),
        ]
        + [both_block, both_block, probe_block, probe_block, window_block],
        out_specs=[grad_block, grad_block, whole(SLOTS, 2, 2, W, W)],
        out_shape=[struct(*PROBE), struct(*PROBE), struct(SLOTS, 2, 2, W, W)],
        scratch_shapes=[
            pltpu.VMEM((SLOTS, W, W), f32),
            pltpu.VMEM((2, W, W), f32),
            pltpu.VMEM((2, W, W), f32),
        ],
        compiler_params=params(),
        cost_estimate=cost(16),
    )(core, counts, even_odd_order(), *tabs, meas, intensity, far, u, mine, other, win)


TY = ("z", "xl")
TX = ("xh", "y", "c")
ZX = ("z", "xl", "xh")
SWAP = [(0, 1), (1, 0)]


def up_perm(count):
    return [(i, i + 1) for i in range(count - 1)]


def down_perm(count):
    return [(i + 1, i) for i in range(count - 1)]


def after(x, *earlier):
    return lax.optimization_barrier((x,) + earlier)[0]


def exchange(x, axes):
    return lax.all_to_all(x, axes, split_axis=0, concat_axis=0, tiled=True)


def body(object_slices, probe_rows, measured, positions, counts):
    tabs = tuple(jnp.asarray(t) for t in make_tables())
    pos = positions[0, 0]
    core = lax.axis_index("c").reshape(1)

    mid = object_slices
    up, down = row_slices(mid)
    probe_rows = after(jnp.broadcast_to(probe_rows[None], (16, 16, W)), up, down)
    probe_rows = exchange(probe_rows, ZX)
    top = lax.ppermute(up, TY, up_perm(8))
    bot = lax.ppermute(down, TY, down_perm(8))
    probe_rows = after(probe_rows, top)
    mine = exchange(jnp.broadcast_to(probe_rows.reshape(1, 256, W), (4, 256, W)), "y")
    mine = mine.reshape(*PROBE)
    meas = exchange(after(measured[0], top), TX)
    right, left = column_slices(mid, top, bot)
    lft = lax.ppermute(right, TX, up_perm(16))
    rgt = lax.ppermute(left, TX, down_perm(16))
    other = lax.ppermute(mine, "c", SWAP)
    lft, rgt, meas = lax.optimization_barrier((lft, rgt, meas))
    win = extract(pos, mid, top, bot, lft, rgt)
    u, farfield, intensity = forward(tabs, core, mine, other, win)
    mine, other, grad_win = backward(
        tabs, 1.0 / 16.0, core, counts, meas, intensity, farfield, u, mine, other, win
    )
    mine = mine + lax.ppermute(other, "c", SWAP)
    mid, top, bot, lft, rgt = place(pos, grad_win)
    from_right = lax.ppermute(lft, TX, down_perm(16))
    from_left = lax.ppermute(rgt, TX, up_perm(16))
    mine = exchange(after(mine.reshape(16, 64, W), lft, rgt), ZX)
    above, below = rims(top, bot, from_right, from_left)
    above_sum = lax.ppermute(below, TY, up_perm(8))
    below_sum = lax.ppermute(above, TY, down_perm(8))
    mine = jnp.sum(after(mine, above, below), 0).reshape(4, 16, W)
    mine = exchange(mine, "y")
    probe_grad = jnp.sum(mine, 0)
    return combine(mid, from_right, from_left, above_sum, below_sum), probe_grad


def solution(mesh):
    fine = Mesh(mesh.devices.reshape(4, 2, 2, 4, 2), ("z", "xl", "xh", "y", "c"))
    in_specs = (
        P(None, None, TY, TX),
        P(TY + TX, None),
        P(TY, None, None, TX, None),
        P(TY, TX, None, None),
        P(TY, TX),
    )
    out_specs = (P(None, None, TY, TX), P(TY + TX, None))
    return jax.shard_map(
        body, mesh=fine, in_specs=in_specs, out_specs=out_specs, check_vma=False
    )
```

```python
import functools

import jax
import jax.numpy as jnp
import ml_dtypes
import numpy as np
from jax import lax
from jax.experimental import pallas as pl
from jax.experimental.pallas import tpu as pltpu
from jax.sharding import Mesh
from jax.sharding import PartitionSpec as P

W = 256
H = 128
MODES = 4
SLOTS = 2
amp_floor = 0.5
f32 = jnp.float32
bf16 = jnp.bfloat16
VMEM_BYTES = 24 << 20
MAIN_BYTES = 60 << 20


def real_form(a):
    return np.block([[a.real, -a.imag], [a.imag, a.real]])


def make_tables():
    k = np.arange(W)
    dft_matrix = np.exp(-2j * np.pi * ((k[:, None] * k[None, :]) % W) / W) / np.sqrt(W)
    freq = (k + H) % W - H
    phase = np.exp(2j * np.pi * ((freq * freq) % (4 * W)) / (4 * W))
    circ = dft_matrix.conj() @ np.diag(phase) @ dft_matrix
    c0, c1 = circ[:H, :H], circ[H:, :H]
    mats = [(c0 + c1) / 2, (c0 - c1) / 2, dft_matrix[0::2, :H], dft_matrix[1::2, :H]]
    high, low = [], []
    for mat in mats:
        full = real_form(mat)
        for form in (full, full.T):
            top = form.astype(np.float32).astype(ml_dtypes.bfloat16)
            high.append(top)
            low.append((form - top.astype(np.float64)).astype(np.float32).astype(ml_dtypes.bfloat16))
    return np.stack(high), np.stack(low)


def split(x):
    top = x.astype(bf16)
    return top, (x - top.astype(f32)).astype(bf16)


dot = functools.partial(jnp.dot, preferred_element_type=f32)


def left_product(tabs, i, x):
    top, rest = split(x)
    hi, lo = tabs
    return dot(hi[i], top) + dot(lo[i], top) + dot(hi[i], rest)


def right_product(tabs, i, x):
    top, rest = split(x)
    hi, lo = tabs
    return dot(top, hi[i]) + dot(top, lo[i]) + dot(rest, hi[i])


def halves(x, axis):
    return (x[:H], x[H:]) if axis == 0 else (x[:, :H], x[:, H:])


def one_side(tabs, axis, ia, ib, xr, xi, fold_in, fold_out):
    (ar, br), (ai, bi) = halves(xr, axis), halves(xi, axis)
    if fold_in:
        ar, br, ai, bi = ar + br, ar - br, ai + bi, ai - bi
    product = left_product if axis == 0 else right_product
    ya = product(tabs, ia, jnp.concatenate([ar, ai], axis))
    yb = product(tabs, ib, jnp.concatenate([br, bi], axis))
    if fold_out:
        ya, yb = ya + yb, ya - yb
    (ar, ai), (br, bi) = halves(ya, axis), halves(yb, axis)
    return jnp.concatenate([ar, br], axis), jnp.concatenate([ai, bi], axis)


def propagate(tabs, xr, xi, adjoint):
    t = 1 if adjoint else 0
    xr, xi = one_side(tabs, 0, 0 + t, 2 + t, xr, xi, True, True)
    return one_side(tabs, 1, 1 - t, 3 - t, xr, xi, True, True)


def dft(tabs, xr, xi):
    xr, xi = one_side(tabs, 0, 4, 6, xr, xi, True, False)
    return one_side(tabs, 1, 5, 7, xr, xi, True, False)


def dft_adjoint(tabs, xr, xi):
    xr, xi = one_side(tabs, 0, 5, 7, xr, xi, False, True)
    return one_side(tabs, 1, 4, 6, xr, xi, False, True)


def params():
    return pltpu.CompilerParams(vmem_limit_bytes=VMEM_BYTES)


def struct(*shape):
    return jax.ShapeDtypeStruct(shape, f32)


SMEM = pl.BlockSpec(memory_space=pltpu.SMEM)
VMEM = pl.BlockSpec(memory_space=pltpu.VMEM)
HBM = pl.BlockSpec(memory_space=pltpu.HBM)


def cost(transforms):
    return pl.CostEstimate(flops=transforms * 1_200_000_000, bytes_accessed=1 << 20, transcendentals=0)


def rim_starts(where):
    c, xl = where[0], where[2]
    at = lambda flag, one, zero: pl.multiple_of(flag * (one - zero) + zero, H)
    row_near, row_far = at(xl, 0, H + W), at(xl, H + W, 0)
    col_near, col_far = at(c, 0, H + W), at(c, H + W, 0)
    return (row_near, row_far), (col_near, col_far)


def half_starts(where):
    c, xl = where[0], where[2]
    at = lambda flag, one, zero: pl.multiple_of(flag * (one - zero) + zero, H)
    return (at(xl, 0, H), at(xl, H, 0)), (at(c, 0, H), at(c, H, 0))


def row_slices_kernel(where, mid, near, far):
    starts, _ = half_starts(where)
    near[...] = mid[:, :, pl.ds(starts[0], H), :]
    far[...] = mid[:, :, pl.ds(starts[1], H), :]


def row_slices(where, mid):
    block = pl.BlockSpec((1, 2, H, W), lambda j: (j, 0, 0, 0))
    return pl.pallas_call(
        row_slices_kernel,
        grid=(2,),
        in_specs=[SMEM, pl.BlockSpec((1, 2, W, W), lambda j: (j, 0, 0, 0))],
        out_specs=[block, block],
        out_shape=[struct(2, 2, H, W)] * 2,
        compiler_params=params(),
    )(where, mid)


def column_slices_kernel(where, mid, row_near, row_far, near, far):
    rows, _ = rim_starts(where)
    _, cols = half_starts(where)
    for out, col in ((near, cols[0]), (far, cols[1])):
        part = pl.ds(col, H)
        out[:, :, H : H + W] = mid[:, :, :, part]
        out[:, :, pl.ds(rows[0], H)] = row_near[:, :, :, part]
        out[:, :, pl.ds(rows[1], H)] = row_far[:, :, :, part]


def column_slices(where, mid, row_near, row_far):
    rim = pl.BlockSpec((1, 2, H, W), lambda j: (j, 0, 0, 0))
    tall = pl.BlockSpec((1, 2, 2 * W, H), lambda j: (j, 0, 0, 0))
    return pl.pallas_call(
        column_slices_kernel,
        grid=(2,),
        in_specs=[SMEM, pl.BlockSpec((1, 2, W, W), lambda j: (j, 0, 0, 0)), rim, rim],
        out_specs=[tall, tall],
        out_shape=[struct(2, 2, 2 * W, H)] * 2,
        compiler_params=params(),
    )(where, mid, row_near, row_far)


def corner(pos, s):
    r = pos[s, 0]
    c = pos[s, 1]
    rows = pl.ds(pl.multiple_of(r // 8 * 8, 8), W + 8)
    cols = [pl.ds(pl.multiple_of(c // H * H + k * H, H), H) for k in range(3)]
    return rows, cols, r % 8, c % H


def start_all(pairs, sems):
    copies = [pltpu.make_async_copy(a, b, sems.at[k]) for k, (a, b) in enumerate(pairs)]
    for copy in copies:
        copy.start()
    return copies


def wait_all(copies):
    for copy in copies:
        copy.wait()


def rims_kernel(where, row_near, row_far, col_near, col_far, out_near, out_far, rows, sides, sems):
    starts, _ = rim_starts(where)
    _, halves_at = half_starts(where)
    pairs = [(row_near, rows.at[0]), (row_far, rows.at[1])]
    for k in range(2):
        cells = pl.ds(starts[k], H)
        pairs.append((col_near.at[:, :, cells, :], sides.at[2 * k]))
        pairs.append((col_far.at[:, :, cells, :], sides.at[2 * k + 1]))
    wait_all(start_all(pairs, sems))
    for k, out in ((0, out_near), (1, out_far)):
        for i in range(2):
            part = pl.ds(halves_at[i], H)
            out[:, :, :, part] = rows[k, :, :, :, part] + sides[2 * k + i]


def rims(where, row_near, row_far, col_near, col_far):
    return pl.pallas_call(
        rims_kernel,
        in_specs=[SMEM] + [HBM] * 4,
        out_specs=[VMEM] * 2,
        out_shape=[struct(2, 2, H, W)] * 2,
        scratch_shapes=[
            pltpu.VMEM((2, 2, 2, H, W), f32),
            pltpu.VMEM((4, 2, 2, H, H), f32),
            pltpu.SemaphoreType.DMA((6,)),
        ],
        compiler_params=params(),
    )(where, row_near, row_far, col_near, col_far)


def combine_near_kernel(where, mid, col_near, col_far, row_near, out, total, cols, rows, sems, out_sems):
    rows_at, cols_at = half_starts(where)
    inner = pl.ds(H, W)
    copies = []
    for j in range(2):
        pairs = [
            (mid.at[j], total.at[j]),
            (col_near.at[j, :, inner, :], cols.at[j, 0]),
            (col_far.at[j, :, inner, :], cols.at[j, 1]),
            (row_near.at[j], rows.at[j]),
        ]
        copies.append(start_all(pairs, sems.at[j]))
    done = []
    for j in range(2):
        wait_all(copies[j])
        for i in range(2):
            total[j, :, :, pl.ds(cols_at[i], H)] += cols[j, i]
        total[j, :, pl.ds(rows_at[0], H), :] += rows[j]
        done += start_all([(total.at[j], out.at[j])], out_sems.at[pl.ds(j, 1)])
    wait_all(done)


def combine_near(where, mid, col_near, col_far, row_near):
    return pl.pallas_call(
        combine_near_kernel,
        in_specs=[SMEM] + [HBM] * 4,
        out_specs=HBM,
        out_shape=struct(2, 2, W, W),
        scratch_shapes=[
            pltpu.VMEM((2, 2, W, W), f32),
            pltpu.VMEM((2, 2, 2, W, H), f32),
            pltpu.VMEM((2, 2, H, W), f32),
            pltpu.SemaphoreType.DMA((2, 4)),
            pltpu.SemaphoreType.DMA((2,)),
        ],
        compiler_params=params(),
    )(where, mid, col_near, col_far, row_near)


def even_odd_order():
    perm = np.zeros((W, W), ml_dtypes.bfloat16)
    perm[np.arange(W), np.concatenate([np.arange(0, W, 2), np.arange(1, W, 2)])] = 1
    return jnp.asarray(np.stack([perm, perm.T]))


def pieces_of(x):
    out = []
    for _ in range(3):
        out.append(x.astype(bf16))
        x = x - out[-1].astype(f32)
    return out


def reordered(order, x):
    a, b, c = pieces_of(x)
    x = (dot(order[0], a) + dot(order[0], b)) + dot(order[0], c)
    a, b, c = pieces_of(x)
    return (dot(a, order[1]) + dot(b, order[1])) + dot(c, order[1])


PROBE = (4, 4, 4, 16, W)


def block_rows(x, y, c):
    return pl.ds(pl.multiple_of((x % 2) * 128 + y * 32 + c * 16, 16), 16)


def ext_pieces(where, ext, mid, row_near, row_far, col_near, col_far):
    rows, cols = rim_starts(where)
    inner = pl.ds(H, W)
    full = pl.ds(0, 2 * W)
    return [
        (mid, ext.at[:, :, inner, inner]),
        (row_near, ext.at[:, :, pl.ds(rows[0], H), inner]),
        (row_far, ext.at[:, :, pl.ds(rows[1], H), inner]),
        (col_near, ext.at[:, :, full, pl.ds(cols[0], H)]),
        (col_far, ext.at[:, :, full, pl.ds(cols[1], H)]),
    ]


def extract(pos, ext, win):
    lane = lax.broadcasted_iota(jnp.int32, (W + 8, H), 1)
    sub = lax.broadcasted_iota(jnp.int32, (W // 8, 8, H), 1)
    for s in range(SLOTS):
        rows, cols, dr, dc = corner(pos, s)
        for j in range(2):
            for p in range(2):
                turned = [pltpu.roll(ext[j, p, rows, col], (H - dc) % H, 1) for col in cols]
                for k in range(2):
                    x = jnp.where(lane < H - dc, turned[k], turned[k + 1])
                    x = pltpu.roll(x.reshape(W // 8 + 1, 8, H), (8 - dr) % 8, 1)
                    x = jnp.where(sub < 8 - dr, x[:-1], x[1:])
                    win[s, j, p, :, k * H : k * H + H] = x.reshape(W, H)


def place(pos, grad, ext):
    lane = lax.broadcasted_iota(jnp.int32, (W + 8, H), 1)
    sub = lax.broadcasted_iota(jnp.int32, (W // 8 + 1, 8, H), 1)
    group = jnp.zeros((1, 8, H), f32)
    ext[...] = jnp.zeros_like(ext)
    for s in range(SLOTS):
        rows, cols, dr, dc = corner(pos, s)
        for j in range(2):
            for p in range(2):
                turned = []
                for k in range(2):
                    x = grad[s, j, p, :, k * H : k * H + H].reshape(W // 8, 8, H)
                    x = pltpu.roll(x, dr, 1)
                    x = jnp.where(
                        sub >= dr,
                        jnp.concatenate([x, group], 0),
                        jnp.concatenate([group, x], 0),
                    )
                    turned.append(pltpu.roll(x.reshape(W + 8, H), dc, 1))
                ext[j, p, rows, cols[0]] += jnp.where(lane >= dc, turned[0], 0.0)
                ext[j, p, rows, cols[1]] += jnp.where(lane >= dc, turned[1], turned[0])
                ext[j, p, rows, cols[2]] += jnp.where(lane >= dc, 0.0, turned[1])


def forward_step(tabs, probe, win, u, far, intensity, k):
    m, s = k // 2, k % 2
    pr, pi = probe[m, 0], probe[m, 1]
    a, b = win[s, 0, 0], win[s, 0, 1]
    ur, ui = propagate(tabs, pr * a - pi * b, pr * b + pi * a, False)
    u[k, 0] = ur
    u[k, 1] = ui
    a, b = win[s, 1, 0], win[s, 1, 1]
    fr, fi = dft(tabs, ur * a - ui * b, ur * b + ui * a)
    far[k, 0] = fr
    far[k, 1] = fi
    power = fr * fr + fi * fi
    intensity[s] = jnp.where(m == 0, power, intensity[s] + power)


def backward_step(tabs, probe, win, u, far, scale, grad_probe, grad_win, k):
    m, s = k // 2, k % 2
    factor = scale[s]
    gr, gi = dft_adjoint(tabs, factor * far[k, 0], factor * far[k, 1])
    ur, ui = u[k, 0], u[k, 1]
    vr = gr * ur + gi * ui
    vi = gi * ur - gr * ui
    grad_win[s, 1, 0] = jnp.where(m == 0, vr, grad_win[s, 1, 0] + vr)
    grad_win[s, 1, 1] = jnp.where(m == 0, vi, grad_win[s, 1, 1] + vi)
    a, b = win[s, 1, 0], win[s, 1, 1]
    gr, gi = propagate(tabs, gr * a + gi * b, gi * a - gr * b, True)
    pr, pi = probe[m, 0], probe[m, 1]
    wr = gr * pr + gi * pi
    wi = gi * pr - gr * pi
    grad_win[s, 0, 0] = jnp.where(m == 0, wr, grad_win[s, 0, 0] + wr)
    grad_win[s, 0, 1] = jnp.where(m == 0, wi, grad_win[s, 0, 1] + wi)
    a, b = win[s, 0, 0], win[s, 0, 1]
    qr = gr * a + gi * b
    qi = gi * a - gr * b
    grad_probe[m, 0] = jnp.where(s == 0, qr, grad_probe[m, 0] + qr)
    grad_probe[m, 1] = jnp.where(s == 0, qi, grad_probe[m, 1] + qi)


def main_kernel(
    loss_scale, where, pos, counts, order, high, low, mine, other, meas, meas_core, meas_far, meas_far_core,
    mid, row_near, row_far, col_near, col_far,
    out_mine, out_other, out_mid, out_row_near, out_row_far, out_col_near, out_col_far,
    ext, win, probe, u, far, scale, grad_probe, grad_win, blocks, hi, lo, rows, pattern, perm, sems, more_sems,
):
    copies = start_all(ext_pieces(where, ext, mid, row_near, row_far, col_near, col_far), sems)
    c, h, xl = where[0], where[1], where[2]
    pairs = [(high, hi), (low, lo), (mine, blocks.at[0]), (other, blocks.at[1]), (order, perm)]
    pairs += [(meas.at[:, h, c], rows.at[0, 0]), (meas_core, rows.at[0, 1])]
    pairs += [(meas_far.at[:, c], rows.at[1, 0]), (meas_far_core, rows.at[1, 1])]
    more = start_all(pairs, more_sems)
    wait_all(copies)
    extract(pos, ext, win)
    wait_all(more)
    for m in range(MODES):
        for k in range(4):
            x = (2 * xl + h + k) % 4
            for y in range(4):
                probe[m, x // 2, block_rows(x, y, c), :] = blocks[0, m, k, y]
                probe[m, x // 2, block_rows(x, y, 1 - c), :] = blocks[1, m, k, y]
    tabs = (hi, lo)

    def forward(k, _):
        forward_step(tabs, probe, win, u, far, scale, k)
        return 0

    lax.fori_loop(0, MODES * SLOTS, forward, 0)
    for s in range(SLOTS):
        weight = jnp.where(s < counts[0, 0], 2.0 * loss_scale, 0.0)
        for i, half in ((0, h), (1, 1 - h)):
            for k, core in ((0, c), (1, 1 - c)):
                for y in range(4):
                    start = pl.multiple_of(half * H + y * 32 + core * 16, 16)
                    pattern[pl.ds(start, 16), :] = rows[i, k, y, s]
        amplitude = reordered(perm, pattern[...])
        scale[s] = weight * (1.0 - amplitude * lax.rsqrt(scale[s] + amp_floor))

    def backward(k, _):
        backward_step(tabs, probe, win, u, far, scale, grad_probe, grad_win, k)
        return 0

    lax.fori_loop(0, MODES * SLOTS, backward, 0)
    place(pos, grad_win, ext)
    pairs = ext_pieces(where, ext, out_mid, out_row_near, out_row_far, out_col_near, out_col_far)
    copies = start_all([(b, a) for a, b in pairs], sems)
    for m in range(MODES):
        for x in range(4):
            for y in range(4):
                out_mine[m, x, y] = grad_probe[m, x // 2, block_rows(x, y, c), :]
                out_other[m, x, y] = grad_probe[m, x // 2, block_rows(x, y, 1 - c), :]
    wait_all(copies)


def gradients(tabs, loss_scale, where, pos, counts, *arrays):
    steps = MODES * SLOTS
    return pl.pallas_call(
        functools.partial(main_kernel, loss_scale),
        in_specs=[SMEM] * 3 + [HBM] * 14,
        out_specs=[VMEM] * 2 + [HBM] * 5,
        out_shape=[
            struct(*PROBE),
            struct(*PROBE),
            struct(2, 2, W, W),
            struct(2, 2, H, W),
            struct(2, 2, H, W),
            struct(2, 2, 2 * W, H),
            struct(2, 2, 2 * W, H),
        ],
        scratch_shapes=[
            pltpu.VMEM((2, 2, 2 * W, 2 * W), f32),
            pltpu.VMEM((SLOTS, 2, 2, W, W), f32),
            pltpu.VMEM((MODES, 2, W, W), f32),
            pltpu.VMEM((steps, 2, W, W), f32),
            pltpu.VMEM((steps, 2, W, W), f32),
            pltpu.VMEM((SLOTS, W, W), f32),
            pltpu.VMEM((MODES, 2, W, W), f32),
            pltpu.VMEM((SLOTS, 2, 2, W, W), f32),
            pltpu.VMEM((2,) + PROBE, f32),
            pltpu.VMEM((8, W, W), bf16),
            pltpu.VMEM((8, W, W), bf16),
            pltpu.VMEM((2, 2, 4, SLOTS, 16, W), f32),
            pltpu.VMEM((W, W), f32),
            pltpu.VMEM((2, W, W), bf16),
            pltpu.SemaphoreType.DMA((5,)),
            pltpu.SemaphoreType.DMA((9,)),
        ],
        compiler_params=pltpu.CompilerParams(vmem_limit_bytes=MAIN_BYTES),
        cost_estimate=cost(32),
    )(where, pos, counts, even_odd_order(), *tabs, *arrays)


TY = ("z", "xl")
TX = ("xh", "y", "c")
PLANE = ("xl", "xh", "y")
SWAP = [(0, 1), (1, 0)]


def far_pairs(count):
    return [(i, i + 1) for i in range(1, count - 1, 2)] + [(i + 1, i) for i in range(1, count - 1, 2)]


def after(x, *earlier):
    return lax.optimization_barrier((x,) + earlier)[0]


def exchange(x, axes):
    return lax.all_to_all(x, axes, split_axis=0, concat_axis=0, tiled=True)


def pick(x, index, axis):
    return lax.dynamic_index_in_dim(x, index, axis, keepdims=False)


def swap_rows(near, far):
    return lax.ppermute(near, "xl", SWAP), lax.ppermute(far, TY, far_pairs(8))


def swap_columns(near, far):
    return lax.ppermute(near, "c", SWAP), lax.ppermute(far, TX, far_pairs(16))


def body(object_slices, probe_rows, measured, positions, counts):
    tabs = tuple(jnp.asarray(t) for t in make_tables())
    pos = positions[0, 0]
    where = jnp.stack([lax.axis_index(name) for name in ("c", "xh", "xl")])

    mid = object_slices
    near, far = row_slices(where, mid)
    row_near, row_far = swap_rows(near, far)
    tiles = measured.reshape(2, 4, 2, SLOTS, 16, W).transpose(1, 0, 2, 3, 4, 5).reshape(4, 128, W)
    spread = jnp.broadcast_to(probe_rows[None], (4, 16, W))
    both = exchange(after(jnp.concatenate([spread, tiles], 1), near, far), "y")
    probe_rows = both[:, :16].reshape(64, W)
    meas = both[:, 16:].reshape(4, 2, 2, SLOTS, 16, W)
    c, h = where[0], where[1]
    meas_far = lax.ppermute(pick(meas, 1 - h, 1), "xh", SWAP)
    meas_core = lax.ppermute(pick(pick(meas, h, 1), 1 - c, 1), "c", SWAP)
    meas_far_core = lax.ppermute(pick(meas_far, 1 - c, 1), "c", SWAP)
    probe_rows = [probe_rows] + [
        lax.ppermute(probe_rows, ("xl", "xh"), [((i + k) % 4, i) for i in range(4)]) for k in range(1, 4)
    ]
    probe_rows = after(jnp.stack(probe_rows), row_near, row_far)
    mine = exchange(jnp.broadcast_to(probe_rows.reshape(1, 256, W), (4, 256, W)), "z")
    mine = mine.reshape(*PROBE)
    near, far = column_slices(where, mid, row_near, row_far)
    col_near, col_far = swap_columns(near, far)
    other = lax.ppermute(after(mine, meas_far), "c", SWAP)
    mine, other, mid, row_near, row_far, col_near, col_far = gradients(
        tabs, 1.0 / 16.0, where, pos, counts, mine, other, meas, meas_core, meas_far, meas_far_core,
        mid, row_near, row_far, col_near, col_far,
    )
    mine = mine + lax.ppermute(other, "c", SWAP)
    col_near, col_far = swap_columns(col_near, col_far)
    mine = exchange(mine.reshape(4, 256, W), "z")
    near, far = rims(where, row_near, row_far, col_near, col_far)
    row_near, row_far = swap_rows(near, far)
    mine = jnp.sum(after(mine, near, far), 0).reshape(16, 16, W)
    probe_grad = jnp.sum(exchange(mine, PLANE), 0)
    mid = after(mid, mine)
    held = combine_near(where, mid, col_near, col_far, row_near)
    corner_at = (0, 0, where[2] * H, 0)
    far = lax.dynamic_slice(held, corner_at, (2, 2, H, W)) + row_far
    return lax.dynamic_update_slice(held, far, corner_at), probe_grad


def solution(mesh):
    fine = Mesh(mesh.devices.reshape(4, 2, 2, 4, 2), ("z", "xl", "xh", "y", "c"))
    in_specs = (
        P(None, None, TY, TX),
        P(TY + TX, None),
        P(TY, None, None, TX, None),
        P(TY, TX, None, None),
        P(TY, TX),
    )
    out_specs = (P(None, None, TY, TX), P(TY + TX, None))
    return jax.shard_map(
        body, mesh=fine, in_specs=in_specs, out_specs=out_specs, check_vma=False
    )
```

```python
import functools

import jax
import jax.numpy as jnp
import ml_dtypes
import numpy as np
from jax import lax
from jax.experimental import pallas as pl
from jax.experimental.pallas import tpu as pltpu
from jax.sharding import Mesh
from jax.sharding import PartitionSpec as P

W = 256
H = 128
MODES = 4
SLOTS = 2
amp_floor = 0.5
f32 = jnp.float32
bf16 = jnp.bfloat16
VMEM_BYTES = 24 << 20
MAIN_BYTES = 60 << 20


def real_form(a):
    return np.block([[a.real, -a.imag], [a.imag, a.real]])


def make_tables():
    k = np.arange(W)
    dft_matrix = np.exp(-2j * np.pi * ((k[:, None] * k[None, :]) % W) / W) / np.sqrt(W)
    freq = (k + H) % W - H
    phase = np.exp(2j * np.pi * ((freq * freq) % (4 * W)) / (4 * W))
    circ = dft_matrix.conj() @ np.diag(phase) @ dft_matrix
    c0, c1 = circ[:H, :H], circ[H:, :H]
    mats = [(c0 + c1) / 2, (c0 - c1) / 2, dft_matrix[0::2, :H], dft_matrix[1::2, :H]]
    high, low = [], []
    for mat in mats:
        full = real_form(mat)
        for form in (full, full.T):
            top = form.astype(np.float32).astype(ml_dtypes.bfloat16)
            high.append(top)
            low.append((form - top.astype(np.float64)).astype(np.float32).astype(ml_dtypes.bfloat16))
    return np.stack(high), np.stack(low)


def split(x):
    top = x.astype(bf16)
    return top, (x - top.astype(f32)).astype(bf16)


dot = functools.partial(jnp.dot, preferred_element_type=f32)


def left_product(tabs, i, x):
    top, rest = split(x)
    hi, lo = tabs
    y = dot(jnp.concatenate([hi[i], lo[i]], 0), top)
    return y[:W] + (y[W:] + dot(hi[i], rest))


def right_product(tabs, i, x):
    top, rest = split(x)
    hi, lo = tabs
    y = dot(jnp.concatenate([top, rest], 0), hi[i])
    return y[:W] + (y[W:] + dot(top, lo[i]))


def halves(x, axis):
    return (x[:H], x[H:]) if axis == 0 else (x[:, :H], x[:, H:])


def one_field(tabs, axis, ia, ib, field, fold_in, fold_out):
    product = left_product if axis == 0 else right_product
    (ar, br), (ai, bi) = halves(field[0], axis), halves(field[1], axis)
    if fold_in:
        ar, br, ai, bi = ar + br, ar - br, ai + bi, ai - bi
    ya = product(tabs, ia, jnp.concatenate([ar, ai], axis))
    yb = product(tabs, ib, jnp.concatenate([br, bi], axis))
    if fold_out:
        ya, yb = ya + yb, ya - yb
    (ar, ai), (br, bi) = halves(ya, axis), halves(yb, axis)
    return jnp.concatenate([ar, br], axis), jnp.concatenate([ai, bi], axis)


def one_side(tabs, axis, ia, ib, fields, fold_in, fold_out):
    return [one_field(tabs, axis, ia, ib, field, fold_in, fold_out) for field in fields]


def propagate(tabs, fields, adjoint):
    t = 1 if adjoint else 0
    fields = one_side(tabs, 0, 0 + t, 2 + t, fields, True, True)
    return one_side(tabs, 1, 1 - t, 3 - t, fields, True, True)


def dft(tabs, fields):
    fields = one_side(tabs, 0, 4, 6, fields, True, False)
    return one_side(tabs, 1, 5, 7, fields, True, False)


def dft_adjoint(tabs, fields):
    fields = one_side(tabs, 0, 5, 7, fields, False, True)
    return one_side(tabs, 1, 4, 6, fields, False, True)


def params():
    return pltpu.CompilerParams(vmem_limit_bytes=VMEM_BYTES)


def struct(*shape):
    return jax.ShapeDtypeStruct(shape, f32)


SMEM = pl.BlockSpec(memory_space=pltpu.SMEM)
VMEM = pl.BlockSpec(memory_space=pltpu.VMEM)
HBM = pl.BlockSpec(memory_space=pltpu.HBM)


def cost(transforms):
    return pl.CostEstimate(flops=transforms * 1_200_000_000, bytes_accessed=1 << 20, transcendentals=0)


def rim_starts(where):
    c, xl = where[0], where[2]
    at = lambda flag, one, zero: pl.multiple_of(flag * (one - zero) + zero, H)
    row_near, row_far = at(xl, 0, H + W), at(xl, H + W, 0)
    col_near, col_far = at(c, 0, H + W), at(c, H + W, 0)
    return (row_near, row_far), (col_near, col_far)


def half_starts(where):
    c, xl = where[0], where[2]
    at = lambda flag, one, zero: pl.multiple_of(flag * (one - zero) + zero, H)
    return (at(xl, 0, H), at(xl, H, 0)), (at(c, 0, H), at(c, H, 0))


def row_slices_kernel(where, mid, near, far):
    starts, _ = half_starts(where)
    near[...] = mid[:, :, pl.ds(starts[0], H), :]
    far[...] = mid[:, :, pl.ds(starts[1], H), :]


def row_slices(where, mid):
    block = pl.BlockSpec((1, 2, H, W), lambda j: (j, 0, 0, 0))
    return pl.pallas_call(
        row_slices_kernel,
        grid=(2,),
        in_specs=[SMEM, pl.BlockSpec((1, 2, W, W), lambda j: (j, 0, 0, 0))],
        out_specs=[block, block],
        out_shape=[struct(2, 2, H, W)] * 2,
        compiler_params=params(),
    )(where, mid)


def column_slices_kernel(where, mid, row_near, row_far, near, far):
    rows, _ = rim_starts(where)
    _, cols = half_starts(where)
    for out, col in ((near, cols[0]), (far, cols[1])):
        part = pl.ds(col, H)
        out[:, :, H : H + W] = mid[:, :, :, part]
        out[:, :, pl.ds(rows[0], H)] = row_near[:, :, :, part]
        out[:, :, pl.ds(rows[1], H)] = row_far[:, :, :, part]


def column_slices(where, mid, row_near, row_far):
    rim = pl.BlockSpec((1, 2, H, W), lambda j: (j, 0, 0, 0))
    tall = pl.BlockSpec((1, 2, 2 * W, H), lambda j: (j, 0, 0, 0))
    return pl.pallas_call(
        column_slices_kernel,
        grid=(2,),
        in_specs=[SMEM, pl.BlockSpec((1, 2, W, W), lambda j: (j, 0, 0, 0)), rim, rim],
        out_specs=[tall, tall],
        out_shape=[struct(2, 2, 2 * W, H)] * 2,
        compiler_params=params(),
    )(where, mid, row_near, row_far)


def corner(pos, s):
    r = pos[s, 0]
    c = pos[s, 1]
    rows = pl.ds(pl.multiple_of(r // 8 * 8, 8), W + 8)
    cols = [pl.ds(pl.multiple_of(c // H * H + k * H, H), H) for k in range(3)]
    return rows, cols, r % 8, c % H


def start_all(pairs, sems):
    copies = [pltpu.make_async_copy(a, b, sems.at[k]) for k, (a, b) in enumerate(pairs)]
    for copy in copies:
        copy.start()
    return copies


def wait_all(copies):
    for copy in copies:
        copy.wait()


def rims_kernel(where, row_near, row_far, col_near, col_far, out_near, out_far, rows, sides, sems):
    starts, _ = rim_starts(where)
    _, halves_at = half_starts(where)
    pairs = [(row_near, rows.at[0]), (row_far, rows.at[1])]
    for k in range(2):
        cells = pl.ds(starts[k], H)
        pairs.append((col_near.at[:, :, cells, :], sides.at[2 * k]))
        pairs.append((col_far.at[:, :, cells, :], sides.at[2 * k + 1]))
    wait_all(start_all(pairs, sems))
    for k, out in ((0, out_near), (1, out_far)):
        for i in range(2):
            part = pl.ds(halves_at[i], H)
            out[:, :, :, part] = rows[k, :, :, :, part] + sides[2 * k + i]


def rims(where, row_near, row_far, col_near, col_far):
    return pl.pallas_call(
        rims_kernel,
        in_specs=[SMEM] + [HBM] * 4,
        out_specs=[VMEM] * 2,
        out_shape=[struct(2, 2, H, W)] * 2,
        scratch_shapes=[
            pltpu.VMEM((2, 2, 2, H, W), f32),
            pltpu.VMEM((4, 2, 2, H, H), f32),
            pltpu.SemaphoreType.DMA((6,)),
        ],
        compiler_params=params(),
    )(where, row_near, row_far, col_near, col_far)


def combine_near_kernel(where, mid, col_near, col_far, row_near, out, total, cols, rows, sems, out_sems):
    rows_at, cols_at = half_starts(where)
    inner = pl.ds(H, W)
    copies = []
    for j in range(2):
        pairs = [
            (mid.at[j], total.at[j]),
            (col_near.at[j, :, inner, :], cols.at[j, 0]),
            (col_far.at[j, :, inner, :], cols.at[j, 1]),
            (row_near.at[j], rows.at[j]),
        ]
        copies.append(start_all(pairs, sems.at[j]))
    done = []
    for j in range(2):
        wait_all(copies[j])
        for i in range(2):
            total[j, :, :, pl.ds(cols_at[i], H)] += cols[j, i]
        total[j, :, pl.ds(rows_at[0], H), :] += rows[j]
        done += start_all([(total.at[j], out.at[j])], out_sems.at[pl.ds(j, 1)])
    wait_all(done)


def combine_near(where, mid, col_near, col_far, row_near):
    return pl.pallas_call(
        combine_near_kernel,
        in_specs=[SMEM] + [HBM] * 4,
        out_specs=HBM,
        out_shape=struct(2, 2, W, W),
        scratch_shapes=[
            pltpu.VMEM((2, 2, W, W), f32),
            pltpu.VMEM((2, 2, 2, W, H), f32),
            pltpu.VMEM((2, 2, H, W), f32),
            pltpu.SemaphoreType.DMA((2, 4)),
            pltpu.SemaphoreType.DMA((2,)),
        ],
        compiler_params=params(),
    )(where, mid, col_near, col_far, row_near)


def even_odd_order():
    perm = np.zeros((W, W), ml_dtypes.bfloat16)
    perm[np.arange(W), np.concatenate([np.arange(0, W, 2), np.arange(1, W, 2)])] = 1
    return jnp.asarray(np.stack([perm, perm.T]))


def pieces_of(x):
    out = []
    for _ in range(3):
        out.append(x.astype(bf16))
        x = x - out[-1].astype(f32)
    return out


def reordered(order, x):
    a, b, c = pieces_of(x)
    x = (dot(order[0], a) + dot(order[0], b)) + dot(order[0], c)
    a, b, c = pieces_of(x)
    return (dot(a, order[1]) + dot(b, order[1])) + dot(c, order[1])


PROBE = (4, 4, 4, 16, W)


def block_rows(x, y, c):
    return pl.ds(pl.multiple_of((x % 2) * 128 + y * 32 + c * 16, 16), 16)


def ext_pieces(where, ext, mid, row_near, row_far, col_near, col_far):
    rows, cols = rim_starts(where)
    inner = pl.ds(H, W)
    full = pl.ds(0, 2 * W)
    return [
        (mid, ext.at[:, :, inner, inner]),
        (row_near, ext.at[:, :, pl.ds(rows[0], H), inner]),
        (row_far, ext.at[:, :, pl.ds(rows[1], H), inner]),
        (col_near, ext.at[:, :, full, pl.ds(cols[0], H)]),
        (col_far, ext.at[:, :, full, pl.ds(cols[1], H)]),
    ]


def extract(pos, ext, win):
    lane = lax.broadcasted_iota(jnp.int32, (W + 8, H), 1)
    sub = lax.broadcasted_iota(jnp.int32, (W // 8, 8, H), 1)
    for s in range(SLOTS):
        rows, cols, dr, dc = corner(pos, s)
        for j in range(2):
            for p in range(2):
                turned = [pltpu.roll(ext[j, p, rows, col], (H - dc) % H, 1) for col in cols]
                for k in range(2):
                    x = jnp.where(lane < H - dc, turned[k], turned[k + 1])
                    x = pltpu.roll(x.reshape(W // 8 + 1, 8, H), (8 - dr) % 8, 1)
                    x = jnp.where(sub < 8 - dr, x[:-1], x[1:])
                    win[s, j, p, :, k * H : k * H + H] = x.reshape(W, H)


def place(pos, grad, ext, j):
    lane = lax.broadcasted_iota(jnp.int32, (W + 8, H), 1)
    sub = lax.broadcasted_iota(jnp.int32, (W // 8 + 1, 8, H), 1)
    group = jnp.zeros((1, 8, H), f32)
    ext[j] = jnp.zeros(ext.shape[1:], f32)
    for s in range(SLOTS):
        rows, cols, dr, dc = corner(pos, s)
        for p in range(2):
            turned = []
            for k in range(2):
                x = grad[s, j, p, :, k * H : k * H + H].reshape(W // 8, 8, H)
                x = pltpu.roll(x, dr, 1)
                x = jnp.where(
                    sub >= dr,
                    jnp.concatenate([x, group], 0),
                    jnp.concatenate([group, x], 0),
                )
                turned.append(pltpu.roll(x.reshape(W + 8, H), dc, 1))
            ext[j, p, rows, cols[0]] += jnp.where(lane >= dc, turned[0], 0.0)
            ext[j, p, rows, cols[1]] += jnp.where(lane >= dc, turned[1], turned[0])
            ext[j, p, rows, cols[2]] += jnp.where(lane >= dc, 0.0, turned[1])


def times(x, y):
    return x[0] * y[0] - x[1] * y[1], x[0] * y[1] + x[1] * y[0]


def times_conj(x, y):
    return x[0] * y[0] + x[1] * y[1], x[1] * y[0] - x[0] * y[1]


def read(ref, *index):
    return ref[(*index, 0)], ref[(*index, 1)]


def write(ref, value, *index):
    for part in range(2):
        ref[(*index, part)] = value[part]


def add_to(ref, value, first, *index):
    for part in range(2):
        at = (*index, part)
        ref[at] = jnp.where(first, value[part], ref[at] + value[part])


def forward_step(tabs, probe, win, u, far, intensity, m):
    slots = range(SLOTS)
    here = read(probe, m)
    fields = propagate(tabs, [times(here, read(win, s, 0)) for s in slots], False)
    for s in slots:
        write(u, fields[s], m, s)
    fields = dft(tabs, [times(fields[s], read(win, s, 1)) for s in slots])
    for s in slots:
        write(far, fields[s], m, s)
        power = fields[s][0] * fields[s][0] + fields[s][1] * fields[s][1]
        intensity[s] = jnp.where(m == 0, power, intensity[s] + power)


def backward_step(tabs, probe, win, u, far, scale, grad_probe, grad_win, m, between):
    slots = range(SLOTS)
    fields = [tuple(scale[s] * part for part in read(far, m, s)) for s in slots]
    fields = dft_adjoint(tabs, fields)
    for s in slots:
        add_to(grad_win, times_conj(fields[s], read(u, m, s)), m == 0, s, 1)
    between()
    fields = propagate(tabs, [times_conj(fields[s], read(win, s, 1)) for s in slots], True)
    here = read(probe, m)
    for s in slots:
        add_to(grad_win, times_conj(fields[s], here), m == 0, s, 0)
    terms = [times_conj(fields[s], read(win, s, 0)) for s in slots]
    write(grad_probe, tuple(a + b for a, b in zip(*terms)))


def main_kernel(
    loss_scale, where, pos, counts, order, high, low, mine, other, meas, meas_core, meas_far, meas_far_core,
    mid, row_near, row_far, col_near, col_far,
    out_mine, out_other, out_mid, out_row_near, out_row_far, out_col_near, out_col_far,
    ext, win, probe, u, far, scale, grad_probe, grad_win, blocks, out_blocks, hi, lo, rows, pattern, perm,
    meas_sems, ext_sems, table_sems, probe_sems, out_sems,
):
    c, h, xl = where[0], where[1], where[2]
    pairs = [(meas.at[:, h, c], rows.at[0, 0]), (meas_core, rows.at[0, 1])]
    pairs += [(meas_far.at[:, c], rows.at[1, 0]), (meas_far_core, rows.at[1, 1]), (order, perm)]
    meas_copies = start_all(pairs, meas_sems)
    ext_copies = start_all(ext_pieces(where, ext, mid, row_near, row_far, col_near, col_far), ext_sems)
    table_copies = start_all([(high, hi), (low, lo)], table_sems)

    def probe_copies(m):
        pairs = ((mine, 0), (other, 1))
        return [pltpu.make_async_copy(a.at[m], blocks.at[k, m], probe_sems.at[m, k]) for a, k in pairs]

    for m in range(MODES):
        for copy in probe_copies(m):
            copy.start()
    wait_all(meas_copies)
    for s in range(SLOTS):
        for i, half in ((0, h), (1, 1 - h)):
            for k, core in ((0, c), (1, 1 - c)):
                for y in range(4):
                    start = pl.multiple_of(half * H + y * 32 + core * 16, 16)
                    pattern[s, pl.ds(start, 16), :] = rows[i, k, y, s]
        pattern[s] = reordered(perm, pattern[s])
    wait_all(ext_copies)
    extract(pos, ext, win)
    wait_all(table_copies)
    tabs = (hi, lo)

    def forward(m, _):
        wait_all(probe_copies(m))
        for k in range(4):
            x = (2 * xl + h + k) % 4
            for y in range(4):
                probe[m, x // 2, block_rows(x, y, c), :] = blocks[0, m, k, y]
                probe[m, x // 2, block_rows(x, y, 1 - c), :] = blocks[1, m, k, y]
        forward_step(tabs, probe, win, u, far, scale, m)
        return 0

    lax.fori_loop(0, MODES, forward, 0)
    for s in range(SLOTS):
        weight = jnp.where(s < counts[0, 0], 2.0 * loss_scale, 0.0)
        scale[s] = weight * (1.0 - pattern[s] * lax.rsqrt(scale[s] + amp_floor))

    def out_copies(m):
        pairs = ((out_mine, 0), (out_other, 1))
        return [pltpu.make_async_copy(out_blocks.at[k, m], a.at[m], probe_sems.at[m, k]) for a, k in pairs]

    def backward(m, between):
        backward_step(tabs, probe, win, u, far, scale, grad_probe, grad_win, m, between)
        for x in range(4):
            for y in range(4):
                out_blocks[0, m, x, y] = grad_probe[x // 2, block_rows(x, y, c), :]
                out_blocks[1, m, x, y] = grad_probe[x // 2, block_rows(x, y, 1 - c), :]
        for copy in out_copies(m):
            copy.start()
        return 0

    def place_slice(j):
        place(pos, grad_win, ext, j)
        pairs = ext_pieces(where, ext, out_mid, out_row_near, out_row_far, out_col_near, out_col_far)
        return start_all([(b.at[j], a.at[j]) for a, b in pairs], out_sems.at[j])

    copies = []
    lax.fori_loop(0, MODES - 1, lambda m, _: backward(m, lambda: None), 0)
    backward(MODES - 1, lambda: copies.extend(place_slice(1)))
    copies += place_slice(0)
    for m in range(MODES):
        copies += out_copies(m)
    wait_all(copies)


def gradients(tabs, loss_scale, where, pos, counts, *arrays):
    return pl.pallas_call(
        functools.partial(main_kernel, loss_scale),
        in_specs=[SMEM] * 3 + [HBM] * 14,
        out_specs=[HBM] * 7,
        out_shape=[
            struct(*PROBE),
            struct(*PROBE),
            struct(2, 2, W, W),
            struct(2, 2, H, W),
            struct(2, 2, H, W),
            struct(2, 2, 2 * W, H),
            struct(2, 2, 2 * W, H),
        ],
        scratch_shapes=[
            pltpu.VMEM((2, 2, 2 * W, 2 * W), f32),
            pltpu.VMEM((SLOTS, 2, 2, W, W), f32),
            pltpu.VMEM((MODES, 2, W, W), f32),
            pltpu.VMEM((MODES, SLOTS, 2, W, W), f32),
            pltpu.VMEM((MODES, SLOTS, 2, W, W), f32),
            pltpu.VMEM((SLOTS, W, W), f32),
            pltpu.VMEM((2, W, W), f32),
            pltpu.VMEM((SLOTS, 2, 2, W, W), f32),
            pltpu.VMEM((2,) + PROBE, f32),
            pltpu.VMEM((2,) + PROBE, f32),
            pltpu.VMEM((8, W, W), bf16),
            pltpu.VMEM((8, W, W), bf16),
            pltpu.VMEM((2, 2, 4, SLOTS, 16, W), f32),
            pltpu.VMEM((SLOTS, W, W), f32),
            pltpu.VMEM((2, W, W), bf16),
            pltpu.SemaphoreType.DMA((5,)),
            pltpu.SemaphoreType.DMA((5,)),
            pltpu.SemaphoreType.DMA((2,)),
            pltpu.SemaphoreType.DMA((MODES, 2)),
            pltpu.SemaphoreType.DMA((2, 5)),
        ],
        compiler_params=pltpu.CompilerParams(vmem_limit_bytes=MAIN_BYTES),
        cost_estimate=cost(32),
    )(where, pos, counts, even_odd_order(), *tabs, *arrays)


TY = ("z", "xl")
TX = ("xh", "y", "c")
PLANE = ("xl", "xh", "y")
SWAP = [(0, 1), (1, 0)]


def far_pairs(count):
    return [(i, i + 1) for i in range(1, count - 1, 2)] + [(i + 1, i) for i in range(1, count - 1, 2)]


def after(x, *earlier):
    return lax.optimization_barrier((x,) + earlier)[0]


def exchange(x, axes):
    return lax.all_to_all(x, axes, split_axis=0, concat_axis=0, tiled=True)


def pick(x, index, axis):
    return lax.dynamic_index_in_dim(x, index, axis, keepdims=False)


def swap_rows(near, far):
    return lax.ppermute(near, "xl", SWAP), lax.ppermute(far, TY, far_pairs(8))


def swap_columns(near, far):
    return lax.ppermute(near, "c", SWAP), lax.ppermute(far, TX, far_pairs(16))


def body(object_slices, probe_rows, measured, positions, counts):
    tabs = tuple(jnp.asarray(t) for t in make_tables())
    pos = positions[0, 0]
    where = jnp.stack([lax.axis_index(name) for name in ("c", "xh", "xl")])

    mid = object_slices
    near, far = row_slices(where, mid)
    row_near, row_far = swap_rows(near, far)
    tiles = measured.reshape(2, 4, 2, SLOTS, 16, W).transpose(1, 0, 2, 3, 4, 5).reshape(4, 128, W)
    spread = jnp.broadcast_to(probe_rows[None], (4, 16, W))
    both = exchange(after(jnp.concatenate([spread, tiles], 1), near, far), "y")
    probe_rows = both[:, :16].reshape(64, W)
    meas = both[:, 16:].reshape(4, 2, 2, SLOTS, 16, W)
    c, h = where[0], where[1]
    meas_far = lax.ppermute(pick(meas, 1 - h, 1), "xh", SWAP)
    meas_core = lax.ppermute(pick(pick(meas, h, 1), 1 - c, 1), "c", SWAP)
    meas_far_core = lax.ppermute(pick(meas_far, 1 - c, 1), "c", SWAP)
    probe_rows = [probe_rows] + [
        lax.ppermute(probe_rows, ("xl", "xh"), [((i + k) % 4, i) for i in range(4)]) for k in range(1, 4)
    ]
    probe_rows = after(jnp.stack(probe_rows), row_near, row_far)
    mine = exchange(jnp.broadcast_to(probe_rows.reshape(1, 256, W), (4, 256, W)), "z")
    mine = mine.reshape(*PROBE)
    near, far = column_slices(where, mid, row_near, row_far)
    col_near, col_far = swap_columns(near, far)
    other = lax.ppermute(after(mine, meas_far), "c", SWAP)
    mine, other, mid, row_near, row_far, col_near, col_far = gradients(
        tabs, 1.0 / 16.0, where, pos, counts, mine, other, meas, meas_core, meas_far, meas_far_core,
        mid, row_near, row_far, col_near, col_far,
    )
    mine = mine + lax.ppermute(other, "c", SWAP)
    col_near, col_far = swap_columns(col_near, col_far)
    mine = exchange(mine.reshape(4, 256, W), "z")
    near, far = rims(where, row_near, row_far, col_near, col_far)
    row_near, row_far = swap_rows(near, far)
    mine = jnp.sum(after(mine, near, far), 0).reshape(16, 16, W)
    probe_grad = jnp.sum(exchange(mine, PLANE), 0)
    mid = after(mid, mine)
    held = combine_near(where, mid, col_near, col_far, row_near)
    corner_at = (0, 0, where[2] * H, 0)
    far = lax.dynamic_slice(held, corner_at, (2, 2, H, W)) + row_far
    return lax.dynamic_update_slice(held, far, corner_at), probe_grad


def solution(mesh):
    fine = Mesh(mesh.devices.reshape(4, 2, 2, 4, 2), ("z", "xl", "xh", "y", "c"))
    in_specs = (
        P(None, None, TY, TX),
        P(TY + TX, None),
        P(TY, None, None, TX, None),
        P(TY, TX, None, None),
        P(TY, TX),
    )
    out_specs = (P(None, None, TY, TX), P(TY + TX, None))
    return jax.shard_map(
        body, mesh=fine, in_specs=in_specs, out_specs=out_specs, check_vma=False
    )
```

```python
import functools

import jax
import jax.numpy as jnp
import ml_dtypes
import numpy as np
from jax import lax
from jax.experimental import pallas as pl
from jax.experimental.pallas import tpu as pltpu
from jax.sharding import Mesh
from jax.sharding import PartitionSpec as P

W = 256
H = 128
MODES = 4
SLOTS = 2
amp_floor = 0.5
f32 = jnp.float32
bf16 = jnp.bfloat16
VMEM_BYTES = 24 << 20
MAIN_BYTES = 60 << 20


def real_form(a):
    return np.block([[a.real, -a.imag], [a.imag, a.real]])


def make_tables():
    k = np.arange(W)
    dft_matrix = np.exp(-2j * np.pi * ((k[:, None] * k[None, :]) % W) / W) / np.sqrt(W)
    freq = (k + H) % W - H
    phase = np.exp(2j * np.pi * ((freq * freq) % (4 * W)) / (4 * W))
    circ = dft_matrix.conj() @ np.diag(phase) @ dft_matrix
    c0, c1 = circ[:H, :H], circ[H:, :H]
    mats = [(c0 + c1) / 2, (c0 - c1) / 2, dft_matrix[0::2, :H], dft_matrix[1::2, :H]]
    high, low = [], []
    for mat in mats:
        full = real_form(mat)
        for form in (full, full.T):
            top = form.astype(np.float32).astype(ml_dtypes.bfloat16)
            high.append(top)
            low.append((form - top.astype(np.float64)).astype(np.float32).astype(ml_dtypes.bfloat16))
    return np.stack(high), np.stack(low)


def split(x):
    top = x.astype(bf16)
    return top, (x - top.astype(f32)).astype(bf16)


dot = functools.partial(jnp.dot, preferred_element_type=f32)


def left_product(tabs, i, x):
    top, rest = split(x)
    hi, lo = tabs
    y = dot(jnp.concatenate([hi[i], lo[i]], 0), top)
    return y[:W] + (y[W:] + dot(hi[i], rest))


def right_product(tabs, i, x):
    top, rest = split(x)
    hi, lo = tabs
    y = dot(jnp.concatenate([top, rest], 0), hi[i])
    return y[:W] + (y[W:] + dot(top, lo[i]))


def halves(x, axis):
    return (x[:H], x[H:]) if axis == 0 else (x[:, :H], x[:, H:])


def one_field(tabs, axis, ia, ib, field, fold_in, fold_out):
    product = left_product if axis == 0 else right_product
    (ar, br), (ai, bi) = halves(field[0], axis), halves(field[1], axis)
    if fold_in:
        ar, br, ai, bi = ar + br, ar - br, ai + bi, ai - bi
    ya = product(tabs, ia, jnp.concatenate([ar, ai], axis))
    yb = product(tabs, ib, jnp.concatenate([br, bi], axis))
    if fold_out:
        ya, yb = ya + yb, ya - yb
    (ar, ai), (br, bi) = halves(ya, axis), halves(yb, axis)
    return jnp.concatenate([ar, br], axis), jnp.concatenate([ai, bi], axis)


def one_side(tabs, axis, ia, ib, fields, fold_in, fold_out):
    return [one_field(tabs, axis, ia, ib, field, fold_in, fold_out) for field in fields]


def propagate(tabs, fields, adjoint):
    t = 1 if adjoint else 0
    fields = one_side(tabs, 0, 0 + t, 2 + t, fields, True, True)
    return one_side(tabs, 1, 1 - t, 3 - t, fields, True, True)


def dft(tabs, fields):
    fields = one_side(tabs, 0, 4, 6, fields, True, False)
    return one_side(tabs, 1, 5, 7, fields, True, False)


def dft_adjoint(tabs, fields):
    fields = one_side(tabs, 0, 5, 7, fields, False, True)
    return one_side(tabs, 1, 4, 6, fields, False, True)


def params():
    return pltpu.CompilerParams(vmem_limit_bytes=VMEM_BYTES)


def struct(*shape):
    return jax.ShapeDtypeStruct(shape, f32)


SMEM = pl.BlockSpec(memory_space=pltpu.SMEM)
VMEM = pl.BlockSpec(memory_space=pltpu.VMEM)
HBM = pl.BlockSpec(memory_space=pltpu.HBM)


def cost(transforms):
    return pl.CostEstimate(flops=transforms * 1_200_000_000, bytes_accessed=1 << 20, transcendentals=0)


def rim_starts(where):
    c, xl = where[0], where[2]
    at = lambda flag, one, zero: pl.multiple_of(flag * (one - zero) + zero, H)
    row_near, row_far = at(xl, 0, H + W), at(xl, H + W, 0)
    col_near, col_far = at(c, 0, H + W), at(c, H + W, 0)
    return (row_near, row_far), (col_near, col_far)


def half_starts(where):
    c, xl = where[0], where[2]
    at = lambda flag, one, zero: pl.multiple_of(flag * (one - zero) + zero, H)
    return (at(xl, 0, H), at(xl, H, 0)), (at(c, 0, H), at(c, H, 0))


def row_slices_kernel(where, mid, near, far):
    starts, _ = half_starts(where)
    near[...] = mid[:, :, pl.ds(starts[0], H), :]
    far[...] = mid[:, :, pl.ds(starts[1], H), :]


def row_slices(where, mid):
    block = pl.BlockSpec((1, 2, H, W), lambda j: (j, 0, 0, 0))
    return pl.pallas_call(
        row_slices_kernel,
        grid=(2,),
        in_specs=[SMEM, pl.BlockSpec((1, 2, W, W), lambda j: (j, 0, 0, 0))],
        out_specs=[block, block],
        out_shape=[struct(2, 2, H, W)] * 2,
        compiler_params=params(),
    )(where, mid)


def column_slices_kernel(where, mid, row_near, row_far, near, far):
    rows, _ = rim_starts(where)
    _, cols = half_starts(where)
    for out, col in ((near, cols[0]), (far, cols[1])):
        part = pl.ds(col, H)
        out[:, :, H : H + W] = mid[:, :, :, part]
        out[:, :, pl.ds(rows[0], H)] = row_near[:, :, :, part]
        out[:, :, pl.ds(rows[1], H)] = row_far[:, :, :, part]


def column_slices(where, mid, row_near, row_far):
    rim = pl.BlockSpec((1, 2, H, W), lambda j: (j, 0, 0, 0))
    tall = pl.BlockSpec((1, 2, 2 * W, H), lambda j: (j, 0, 0, 0))
    return pl.pallas_call(
        column_slices_kernel,
        grid=(2,),
        in_specs=[SMEM, pl.BlockSpec((1, 2, W, W), lambda j: (j, 0, 0, 0)), rim, rim],
        out_specs=[tall, tall],
        out_shape=[struct(2, 2, 2 * W, H)] * 2,
        compiler_params=params(),
        cost_estimate=cost(40),
    )(where, mid, row_near, row_far)


def corner(pos, s):
    r = pos[s, 0]
    c = pos[s, 1]
    rows = pl.ds(pl.multiple_of(r // 8 * 8, 8), W + 8)
    cols = [pl.ds(pl.multiple_of(c // H * H + k * H, H), H) for k in range(3)]
    return rows, cols, r % 8, c % H


def start_all(pairs, sems):
    copies = [pltpu.make_async_copy(a, b, sems.at[k]) for k, (a, b) in enumerate(pairs)]
    for copy in copies:
        copy.start()
    return copies


def wait_all(copies):
    for copy in copies:
        copy.wait()


def rims_kernel(where, row_near, row_far, col_near, col_far, out_near, out_far, rows, sides, sems):
    starts, _ = rim_starts(where)
    _, halves_at = half_starts(where)
    pairs = [(row_near, rows.at[0]), (row_far, rows.at[1])]
    for k in range(2):
        cells = pl.ds(starts[k], H)
        pairs.append((col_near.at[:, :, cells, :], sides.at[2 * k]))
        pairs.append((col_far.at[:, :, cells, :], sides.at[2 * k + 1]))
    wait_all(start_all(pairs, sems))
    for k, out in ((0, out_near), (1, out_far)):
        for i in range(2):
            part = pl.ds(halves_at[i], H)
            out[:, :, :, part] = rows[k, :, :, :, part] + sides[2 * k + i]


def rims(where, row_near, row_far, col_near, col_far):
    return pl.pallas_call(
        rims_kernel,
        in_specs=[SMEM] + [HBM] * 4,
        out_specs=[VMEM] * 2,
        out_shape=[struct(2, 2, H, W)] * 2,
        scratch_shapes=[
            pltpu.VMEM((2, 2, 2, H, W), f32),
            pltpu.VMEM((4, 2, 2, H, H), f32),
            pltpu.SemaphoreType.DMA((6,)),
        ],
        compiler_params=params(),
    )(where, row_near, row_far, col_near, col_far)


def combine_near_kernel(where, mid, col_near, col_far, row_near, out, total, cols, rows, sems, out_sems):
    rows_at, cols_at = half_starts(where)
    inner = pl.ds(H, W)
    copies = []
    for j in range(2):
        pairs = [
            (mid.at[j], total.at[j]),
            (col_near.at[j, :, inner, :], cols.at[j, 0]),
            (col_far.at[j, :, inner, :], cols.at[j, 1]),
            (row_near.at[j], rows.at[j]),
        ]
        copies.append(start_all(pairs, sems.at[j]))
    done = []
    for j in range(2):
        wait_all(copies[j])
        for i in range(2):
            total[j, :, :, pl.ds(cols_at[i], H)] += cols[j, i]
        total[j, :, pl.ds(rows_at[0], H), :] += rows[j]
        done += start_all([(total.at[j], out.at[j])], out_sems.at[pl.ds(j, 1)])
    wait_all(done)


def combine_near(where, mid, col_near, col_far, row_near):
    return pl.pallas_call(
        combine_near_kernel,
        in_specs=[SMEM] + [HBM] * 4,
        out_specs=HBM,
        out_shape=struct(2, 2, W, W),
        scratch_shapes=[
            pltpu.VMEM((2, 2, W, W), f32),
            pltpu.VMEM((2, 2, 2, W, H), f32),
            pltpu.VMEM((2, 2, H, W), f32),
            pltpu.SemaphoreType.DMA((2, 4)),
            pltpu.SemaphoreType.DMA((2,)),
        ],
        compiler_params=params(),
    )(where, mid, col_near, col_far, row_near)


def even_odd_order():
    perm = np.zeros((W, W), ml_dtypes.bfloat16)
    perm[np.arange(W), np.concatenate([np.arange(0, W, 2), np.arange(1, W, 2)])] = 1
    return jnp.asarray(np.stack([perm, perm.T]))


def pieces_of(x):
    out = []
    for _ in range(3):
        out.append(x.astype(bf16))
        x = x - out[-1].astype(f32)
    return out


def reordered(order, x):
    a, b, c = pieces_of(x)
    x = (dot(order[0], a) + dot(order[0], b)) + dot(order[0], c)
    a, b, c = pieces_of(x)
    return (dot(a, order[1]) + dot(b, order[1])) + dot(c, order[1])


PROBE = (4, 4, 4, 16, W)


def block_rows(x, y, c):
    return pl.ds(pl.multiple_of((x % 2) * 128 + y * 32 + c * 16, 16), 16)


def ext_pieces(where, ext, mid, row_near, row_far, col_near, col_far):
    rows, cols = rim_starts(where)
    inner = pl.ds(H, W)
    full = pl.ds(0, 2 * W)
    return [
        (mid, ext.at[:, :, inner, inner]),
        (row_near, ext.at[:, :, pl.ds(rows[0], H), inner]),
        (row_far, ext.at[:, :, pl.ds(rows[1], H), inner]),
        (col_near, ext.at[:, :, full, pl.ds(cols[0], H)]),
        (col_far, ext.at[:, :, full, pl.ds(cols[1], H)]),
    ]


def extract(pos, ext, win):
    lane = lax.broadcasted_iota(jnp.int32, (W + 8, H), 1)
    sub = lax.broadcasted_iota(jnp.int32, (W // 8, 8, H), 1)
    for s in range(SLOTS):
        rows, cols, dr, dc = corner(pos, s)
        for j in range(2):
            for p in range(2):
                turned = [pltpu.roll(ext[j, p, rows, col], (H - dc) % H, 1) for col in cols]
                for k in range(2):
                    x = jnp.where(lane < H - dc, turned[k], turned[k + 1])
                    x = pltpu.roll(x.reshape(W // 8 + 1, 8, H), (8 - dr) % 8, 1)
                    x = jnp.where(sub < 8 - dr, x[:-1], x[1:])
                    win[s, j, p, :, k * H : k * H + H] = x.reshape(W, H)


def place(pos, grad, ext, j):
    lane = lax.broadcasted_iota(jnp.int32, (W + 8, H), 1)
    sub = lax.broadcasted_iota(jnp.int32, (W // 8 + 1, 8, H), 1)
    group = jnp.zeros((1, 8, H), f32)
    ext[j] = jnp.zeros(ext.shape[1:], f32)
    for s in range(SLOTS):
        rows, cols, dr, dc = corner(pos, s)
        for p in range(2):
            turned = []
            for k in range(2):
                x = grad[s, j, p, :, k * H : k * H + H].reshape(W // 8, 8, H)
                x = pltpu.roll(x, dr, 1)
                x = jnp.where(
                    sub >= dr,
                    jnp.concatenate([x, group], 0),
                    jnp.concatenate([group, x], 0),
                )
                turned.append(pltpu.roll(x.reshape(W + 8, H), dc, 1))
            ext[j, p, rows, cols[0]] += jnp.where(lane >= dc, turned[0], 0.0)
            ext[j, p, rows, cols[1]] += jnp.where(lane >= dc, turned[1], turned[0])
            ext[j, p, rows, cols[2]] += jnp.where(lane >= dc, 0.0, turned[1])


def times(x, y):
    return x[0] * y[0] - x[1] * y[1], x[0] * y[1] + x[1] * y[0]


def times_conj(x, y):
    return x[0] * y[0] + x[1] * y[1], x[1] * y[0] - x[0] * y[1]


def read(ref, *index):
    return ref[(*index, 0)], ref[(*index, 1)]


def write(ref, value, *index):
    for part in range(2):
        ref[(*index, part)] = value[part]


def add_to(ref, value, *index):
    for part in range(2):
        at = (*index, part)
        ref[at] += value[part]


def forward_step(tabs, probe, win, u, far, intensity, m):
    slots = range(SLOTS)
    here = read(probe, m)
    fields = propagate(tabs, [times(here, read(win, s, 0)) for s in slots], False)
    for s in slots:
        write(u, fields[s], m, s)
    fields = dft(tabs, [times(fields[s], read(win, s, 1)) for s in slots])
    for s in slots:
        write(far, fields[s], m, s)
        power = fields[s][0] * fields[s][0] + fields[s][1] * fields[s][1]
        intensity[s] += power


def backward_step(tabs, probe, win, u, far, scale, grad_probe, grad_win, m, between):
    slots = range(SLOTS)
    fields = [tuple(scale[s] * part for part in read(far, m, s)) for s in slots]
    fields = dft_adjoint(tabs, fields)
    for s in slots:
        add_to(grad_win, times_conj(fields[s], read(u, m, s)), s, 1)
    between()
    fields = propagate(tabs, [times_conj(fields[s], read(win, s, 1)) for s in slots], True)
    here = read(probe, m)
    for s in slots:
        add_to(grad_win, times_conj(fields[s], here), s, 0)
    terms = [times_conj(fields[s], read(win, s, 0)) for s in slots]
    write(grad_probe, tuple(a + b for a, b in zip(*terms)))


def main_kernel(
    loss_scale, where, pos, counts, order, high, low, mine, other, meas, meas_core, meas_far, meas_far_core,
    mid, row_near, row_far, col_near, col_far,
    out_mine, out_other, out_mid, out_row_near, out_row_far, out_col_near, out_col_far,
    ext, win, probe, u, far, scale, grad_probe, grad_win, blocks, out_blocks, hi, lo, rows, pattern, perm,
    meas_sems, ext_sems, table_sems, probe_sems, out_sems,
):
    c, h, xl = where[0], where[1], where[2]
    pairs = [(meas.at[:, h, c], rows.at[0, 0]), (meas_core, rows.at[0, 1])]
    pairs += [(meas_far.at[:, c], rows.at[1, 0]), (meas_far_core, rows.at[1, 1]), (order, perm)]
    meas_copies = start_all(pairs, meas_sems)
    ext_copies = start_all(ext_pieces(where, ext, mid, row_near, row_far, col_near, col_far), ext_sems)
    table_copies = start_all([(high, hi), (low, lo)], table_sems)

    def probe_copies(m):
        pairs = ((mine, 0), (other, 1))
        return [pltpu.make_async_copy(a.at[m], blocks.at[k, m], probe_sems.at[m, k]) for a, k in pairs]

    for m in range(MODES):
        for copy in probe_copies(m):
            copy.start()
    scale[...] = jnp.zeros_like(scale)
    grad_win[...] = jnp.zeros_like(grad_win)
    wait_all(meas_copies)
    for s in range(SLOTS):
        for i, half in ((0, h), (1, 1 - h)):
            for k, core in ((0, c), (1, 1 - c)):
                for y in range(4):
                    start = pl.multiple_of(half * H + y * 32 + core * 16, 16)
                    pattern[s, pl.ds(start, 16), :] = rows[i, k, y, s]
        pattern[s] = reordered(perm, pattern[s])
    wait_all(ext_copies)
    extract(pos, ext, win)
    wait_all(table_copies)
    tabs = (hi, lo)

    def forward(m, _):
        wait_all(probe_copies(m))
        for k in range(4):
            x = (2 * xl + h + k) % 4
            for y in range(4):
                probe[m, x // 2, block_rows(x, y, c), :] = blocks[0, m, k, y]
                probe[m, x // 2, block_rows(x, y, 1 - c), :] = blocks[1, m, k, y]
        forward_step(tabs, probe, win, u, far, scale, m)
        return 0

    lax.fori_loop(0, MODES, forward, 0, unroll=2)
    for s in range(SLOTS):
        weight = jnp.where(s < counts[0, 0], 2.0 * loss_scale, 0.0)
        scale[s] = weight * (1.0 - pattern[s] * lax.rsqrt(scale[s] + amp_floor))

    def out_copies(m):
        pairs = ((out_mine, 0), (out_other, 1))
        return [pltpu.make_async_copy(out_blocks.at[k, m], a.at[m], probe_sems.at[m, k]) for a, k in pairs]

    def backward(m, between):
        backward_step(tabs, probe, win, u, far, scale, grad_probe, grad_win, m, between)
        for x in range(4):
            for y in range(4):
                out_blocks[0, m, x, y] = grad_probe[x // 2, block_rows(x, y, c), :]
                out_blocks[1, m, x, y] = grad_probe[x // 2, block_rows(x, y, 1 - c), :]
        for copy in out_copies(m):
            copy.start()
        return 0

    def place_slice(j):
        place(pos, grad_win, ext, j)
        pairs = ext_pieces(where, ext, out_mid, out_row_near, out_row_far, out_col_near, out_col_far)
        return start_all([(b.at[j], a.at[j]) for a, b in pairs], out_sems.at[j])

    copies = []
    lax.fori_loop(0, MODES - 1, lambda m, _: backward(m, lambda: None), 0, unroll=3)
    backward(MODES - 1, lambda: copies.extend(place_slice(1)))
    copies += place_slice(0)
    for m in range(MODES):
        copies += out_copies(m)
    wait_all(copies)


def gradients(tabs, loss_scale, where, pos, counts, *arrays):
    return pl.pallas_call(
        functools.partial(main_kernel, loss_scale),
        in_specs=[SMEM] * 3 + [HBM] * 14,
        out_specs=[HBM] * 7,
        out_shape=[
            struct(*PROBE),
            struct(*PROBE),
            struct(2, 2, W, W),
            struct(2, 2, H, W),
            struct(2, 2, H, W),
            struct(2, 2, 2 * W, H),
            struct(2, 2, 2 * W, H),
        ],
        scratch_shapes=[
            pltpu.VMEM((2, 2, 2 * W, 2 * W), f32),
            pltpu.VMEM((SLOTS, 2, 2, W, W), f32),
            pltpu.VMEM((MODES, 2, W, W), f32),
            pltpu.VMEM((MODES, SLOTS, 2, W, W), f32),
            pltpu.VMEM((MODES, SLOTS, 2, W, W), f32),
            pltpu.VMEM((SLOTS, W, W), f32),
            pltpu.VMEM((2, W, W), f32),
            pltpu.VMEM((SLOTS, 2, 2, W, W), f32),
            pltpu.VMEM((2,) + PROBE, f32),
            pltpu.VMEM((2,) + PROBE, f32),
            pltpu.VMEM((8, W, W), bf16),
            pltpu.VMEM((8, W, W), bf16),
            pltpu.VMEM((2, 2, 4, SLOTS, 16, W), f32),
            pltpu.VMEM((SLOTS, W, W), f32),
            pltpu.VMEM((2, W, W), bf16),
            pltpu.SemaphoreType.DMA((5,)),
            pltpu.SemaphoreType.DMA((5,)),
            pltpu.SemaphoreType.DMA((2,)),
            pltpu.SemaphoreType.DMA((MODES, 2)),
            pltpu.SemaphoreType.DMA((2, 5)),
        ],
        compiler_params=pltpu.CompilerParams(vmem_limit_bytes=MAIN_BYTES),
        cost_estimate=cost(32),
    )(where, pos, counts, even_odd_order(), *tabs, *arrays)


TY = ("z", "xl")
TX = ("xh", "y", "c")
PLANE = ("xl", "xh", "y")
SWAP = [(0, 1), (1, 0)]


def far_pairs(count):
    return [(i, i + 1) for i in range(1, count - 1, 2)] + [(i + 1, i) for i in range(1, count - 1, 2)]


def after(x, *earlier):
    return lax.optimization_barrier((x,) + earlier)[0]


def exchange(x, axes):
    return lax.all_to_all(x, axes, split_axis=0, concat_axis=0, tiled=True)


def pick(x, index, axis):
    return lax.dynamic_index_in_dim(x, index, axis, keepdims=False)


def swap_rows(near, far):
    return lax.ppermute(near, "xl", SWAP), lax.ppermute(far, TY, far_pairs(8))


def swap_columns(near, far):
    return lax.ppermute(near, "c", SWAP), lax.ppermute(far, TX, far_pairs(16))


def body(object_slices, probe_rows, measured, positions, counts):
    tabs = tuple(jnp.asarray(t) for t in make_tables())
    pos = positions[0, 0]
    where = jnp.stack([lax.axis_index(name) for name in ("c", "xh", "xl")])

    mid = object_slices
    near, far = row_slices(where, mid)
    row_near, row_far = swap_rows(near, far)
    tiles = measured.reshape(2, 4, 2, SLOTS, 16, W).transpose(1, 0, 2, 3, 4, 5).reshape(4, 128, W)
    spread = jnp.broadcast_to(probe_rows[None], (4, 16, W))
    both = exchange(after(jnp.concatenate([spread, tiles], 1), near, far), "y")
    probe_rows = both[:, :16].reshape(64, W)
    meas = both[:, 16:].reshape(4, 2, 2, SLOTS, 16, W)
    c, h = where[0], where[1]
    meas_far = lax.ppermute(pick(meas, 1 - h, 1), "xh", SWAP)
    meas_core = lax.ppermute(pick(pick(meas, h, 1), 1 - c, 1), "c", SWAP)
    meas_far_core = lax.ppermute(pick(meas_far, 1 - c, 1), "c", SWAP)
    probe_rows = [probe_rows] + [
        lax.ppermute(probe_rows, ("xl", "xh"), [((i + k) % 4, i) for i in range(4)]) for k in range(1, 4)
    ]
    probe_rows = after(jnp.stack(probe_rows), row_near, row_far)
    mine = exchange(jnp.broadcast_to(probe_rows.reshape(1, 256, W), (4, 256, W)), "z")
    mine = mine.reshape(*PROBE)
    near, far = column_slices(where, mid, row_near, row_far)
    col_near, col_far = swap_columns(near, far)
    other = lax.ppermute(after(mine, meas_far), "c", SWAP)
    mine, other, mid, row_near, row_far, col_near, col_far = gradients(
        tabs, 1.0 / 16.0, where, pos, counts, mine, other, meas, meas_core, meas_far, meas_far_core,
        mid, row_near, row_far, col_near, col_far,
    )
    mine = mine + lax.ppermute(other, "c", SWAP)
    col_near, col_far = swap_columns(col_near, col_far)
    mine = exchange(mine.reshape(4, 256, W), "z")
    near, far = rims(where, row_near, row_far, col_near, col_far)
    row_near, row_far = swap_rows(near, far)
    mine = jnp.sum(after(mine, near, far), 0).reshape(4, 4, 16, W).swapaxes(0, 1)
    total = jnp.sum(exchange(mine, "y"), 0)
    x = 2 * where[2] + h
    parts = [
        lax.ppermute(pick(total, (x + k) % 4, 0), ("xl", "xh"), [(i, (i + k) % 4) for i in range(4)])
        for k in range(1, 4)
    ]
    probe_grad = pick(total, x, 0) + parts[0] + parts[1] + parts[2]
    mid = after(mid, mine)
    held = combine_near(where, mid, col_near, col_far, row_near)
    corner_at = (0, 0, where[2] * H, 0)
    far = lax.dynamic_slice(held, corner_at, (2, 2, H, W)) + row_far
    return lax.dynamic_update_slice(held, far, corner_at), probe_grad


def solution(mesh):
    fine = Mesh(mesh.devices.reshape(4, 2, 2, 4, 2), ("z", "xl", "xh", "y", "c"))
    in_specs = (
        P(None, None, TY, TX),
        P(TY + TX, None),
        P(TY, None, None, TX, None),
        P(TY, TX, None, None),
        P(TY, TX),
    )
    out_specs = (P(None, None, TY, TX), P(TY + TX, None))
    return jax.shard_map(
        body, mesh=fine, in_specs=in_specs, out_specs=out_specs, check_vma=False
    )
```

```python
import functools

import jax
import jax.numpy as jnp
import ml_dtypes
import numpy as np
from jax import lax
from jax.experimental import pallas as pl
from jax.experimental.pallas import tpu as pltpu
from jax.sharding import Mesh
from jax.sharding import PartitionSpec as P

W = 256
H = 128
MODES = 4
SLOTS = 2
amp_floor = 0.5
f32 = jnp.float32
bf16 = jnp.bfloat16
VMEM_BYTES = 24 << 20
MAIN_BYTES = 60 << 20


def real_form(a):
    return np.block([[a.real, -a.imag], [a.imag, a.real]])


def make_tables():
    k = np.arange(W)
    dft_matrix = np.exp(-2j * np.pi * ((k[:, None] * k[None, :]) % W) / W) / np.sqrt(W)
    freq = (k + H) % W - H
    phase = np.exp(2j * np.pi * ((freq * freq) % (4 * W)) / (4 * W))
    circ = dft_matrix.conj() @ np.diag(phase) @ dft_matrix
    c0, c1 = circ[:H, :H], circ[H:, :H]
    mats = [(c0 + c1) / 2, (c0 - c1) / 2, dft_matrix[0::2, :H], dft_matrix[1::2, :H]]
    high, low = [], []
    for mat in mats:
        full = real_form(mat)
        for form in (full, full.T):
            top = form.astype(np.float32).astype(ml_dtypes.bfloat16)
            high.append(top)
            low.append((form - top.astype(np.float64)).astype(np.float32).astype(ml_dtypes.bfloat16))
    return np.stack(high), np.stack(low)


def split(x):
    top = x.astype(bf16)
    return top, (x - top.astype(f32)).astype(bf16)


dot = functools.partial(jnp.dot, preferred_element_type=f32)


def left_product(tabs, i, x):
    top, rest = split(x)
    hi, lo = tabs
    y = dot(jnp.concatenate([hi[i], lo[i]], 0), top)
    return y[:W] + (y[W:] + dot(hi[i], rest))


def right_product(tabs, i, x):
    top, rest = split(x)
    hi, lo = tabs
    y = dot(jnp.concatenate([top, rest], 0), hi[i])
    return y[:W] + (y[W:] + dot(top, lo[i]))


def halves(x, axis):
    return (x[:H], x[H:]) if axis == 0 else (x[:, :H], x[:, H:])


def one_field(tabs, axis, ia, ib, field, fold_in, fold_out):
    product = left_product if axis == 0 else right_product
    (ar, br), (ai, bi) = halves(field[0], axis), halves(field[1], axis)
    if fold_in:
        ar, br, ai, bi = ar + br, ar - br, ai + bi, ai - bi
    ya = product(tabs, ia, jnp.concatenate([ar, ai], axis))
    yb = product(tabs, ib, jnp.concatenate([br, bi], axis))
    if fold_out:
        ya, yb = ya + yb, ya - yb
    (ar, ai), (br, bi) = halves(ya, axis), halves(yb, axis)
    return jnp.concatenate([ar, br], axis), jnp.concatenate([ai, bi], axis)


def one_side(tabs, axis, ia, ib, fields, fold_in, fold_out):
    return [one_field(tabs, axis, ia, ib, field, fold_in, fold_out) for field in fields]


def propagate(tabs, fields, adjoint):
    t = 1 if adjoint else 0
    fields = one_side(tabs, 0, 0 + t, 2 + t, fields, True, True)
    return one_side(tabs, 1, 1 - t, 3 - t, fields, True, True)


def dft(tabs, fields):
    fields = one_side(tabs, 0, 4, 6, fields, True, False)
    return one_side(tabs, 1, 5, 7, fields, True, False)


def dft_adjoint(tabs, fields):
    fields = one_side(tabs, 0, 5, 7, fields, False, True)
    return one_side(tabs, 1, 4, 6, fields, False, True)


def params():
    return pltpu.CompilerParams(vmem_limit_bytes=VMEM_BYTES)


def struct(*shape):
    return jax.ShapeDtypeStruct(shape, f32)


SMEM = pl.BlockSpec(memory_space=pltpu.SMEM)
VMEM = pl.BlockSpec(memory_space=pltpu.VMEM)
HBM = pl.BlockSpec(memory_space=pltpu.HBM)


def cost(transforms):
    return pl.CostEstimate(flops=transforms * 1_200_000_000, bytes_accessed=1 << 20, transcendentals=0)


def rim_starts(where):
    c, xl = where[0], where[2]
    at = lambda flag, one, zero: pl.multiple_of(flag * (one - zero) + zero, H)
    row_near, row_far = at(xl, 0, H + W), at(xl, H + W, 0)
    col_near, col_far = at(c, 0, H + W), at(c, H + W, 0)
    return (row_near, row_far), (col_near, col_far)


def half_starts(where):
    c, xl = where[0], where[2]
    at = lambda flag, one, zero: pl.multiple_of(flag * (one - zero) + zero, H)
    return (at(xl, 0, H), at(xl, H, 0)), (at(c, 0, H), at(c, H, 0))


def row_slices_kernel(where, mid, near, far):
    starts, _ = half_starts(where)
    near[...] = mid[:, :, pl.ds(starts[0], H), :]
    far[...] = mid[:, :, pl.ds(starts[1], H), :]


def row_slices(where, mid):
    block = pl.BlockSpec((1, 2, H, W), lambda j: (j, 0, 0, 0))
    return pl.pallas_call(
        row_slices_kernel,
        grid=(2,),
        in_specs=[SMEM, pl.BlockSpec((1, 2, W, W), lambda j: (j, 0, 0, 0))],
        out_specs=[block, block],
        out_shape=[struct(2, 2, H, W)] * 2,
        compiler_params=params(),
    )(where, mid)


def column_slices_kernel(where, mid, row_near, row_far, near, far):
    rows, _ = rim_starts(where)
    _, cols = half_starts(where)
    for out, col in ((near, cols[0]), (far, cols[1])):
        part = pl.ds(col, H)
        out[:, :, H : H + W] = mid[:, :, :, part]
        out[:, :, pl.ds(rows[0], H)] = row_near[:, :, :, part]
        out[:, :, pl.ds(rows[1], H)] = row_far[:, :, :, part]


def column_slices(where, mid, row_near, row_far):
    rim = pl.BlockSpec((1, 2, H, W), lambda j: (j, 0, 0, 0))
    tall = pl.BlockSpec((1, 2, 2 * W, H), lambda j: (j, 0, 0, 0))
    return pl.pallas_call(
        column_slices_kernel,
        grid=(2,),
        in_specs=[SMEM, pl.BlockSpec((1, 2, W, W), lambda j: (j, 0, 0, 0)), rim, rim],
        out_specs=[tall, tall],
        out_shape=[struct(2, 2, 2 * W, H)] * 2,
        compiler_params=params(),
        cost_estimate=cost(40),
    )(where, mid, row_near, row_far)


def corner(pos, s):
    r = pos[s, 0]
    c = pos[s, 1]
    rows = pl.ds(pl.multiple_of(r // 8 * 8, 8), W + 8)
    cols = [pl.ds(pl.multiple_of(c // H * H + k * H, H), H) for k in range(3)]
    return rows, cols, r % 8, c % H


def start_all(pairs, sems):
    copies = [pltpu.make_async_copy(a, b, sems.at[k]) for k, (a, b) in enumerate(pairs)]
    for copy in copies:
        copy.start()
    return copies


def wait_all(copies):
    for copy in copies:
        copy.wait()


def rims_kernel(where, row_near, row_far, col_near, col_far, out_near, out_far, rows, sides, sems):
    starts, _ = rim_starts(where)
    _, halves_at = half_starts(where)
    pairs = [(row_near, rows.at[0]), (row_far, rows.at[1])]
    for k in range(2):
        cells = pl.ds(starts[k], H)
        pairs.append((col_near.at[:, :, cells, :], sides.at[2 * k]))
        pairs.append((col_far.at[:, :, cells, :], sides.at[2 * k + 1]))
    wait_all(start_all(pairs, sems))
    for k, out in ((0, out_near), (1, out_far)):
        for i in range(2):
            part = pl.ds(halves_at[i], H)
            out[:, :, :, part] = rows[k, :, :, :, part] + sides[2 * k + i]


def rims(where, row_near, row_far, col_near, col_far):
    return pl.pallas_call(
        rims_kernel,
        in_specs=[SMEM] + [HBM] * 4,
        out_specs=[VMEM] * 2,
        out_shape=[struct(2, 2, H, W)] * 2,
        scratch_shapes=[
            pltpu.VMEM((2, 2, 2, H, W), f32),
            pltpu.VMEM((4, 2, 2, H, H), f32),
            pltpu.SemaphoreType.DMA((6,)),
        ],
        compiler_params=params(),
        cost_estimate=cost(40),
    )(where, row_near, row_far, col_near, col_far)


def combine_near_kernel(where, mid, col_near, col_far, row_near, out, total, cols, rows, sems, out_sems):
    rows_at, cols_at = half_starts(where)
    inner = pl.ds(H, W)
    copies = []
    for j in range(2):
        pairs = [
            (mid.at[j], total.at[j]),
            (col_near.at[j, :, inner, :], cols.at[j, 0]),
            (col_far.at[j, :, inner, :], cols.at[j, 1]),
            (row_near.at[j], rows.at[j]),
        ]
        copies.append(start_all(pairs, sems.at[j]))
    done = []
    for j in range(2):
        wait_all(copies[j])
        for i in range(2):
            total[j, :, :, pl.ds(cols_at[i], H)] += cols[j, i]
        total[j, :, pl.ds(rows_at[0], H), :] += rows[j]
        done += start_all([(total.at[j], out.at[j])], out_sems.at[pl.ds(j, 1)])
    wait_all(done)


def combine_near(where, mid, col_near, col_far, row_near):
    return pl.pallas_call(
        combine_near_kernel,
        in_specs=[SMEM] + [HBM] * 4,
        out_specs=HBM,
        out_shape=struct(2, 2, W, W),
        scratch_shapes=[
            pltpu.VMEM((2, 2, W, W), f32),
            pltpu.VMEM((2, 2, 2, W, H), f32),
            pltpu.VMEM((2, 2, H, W), f32),
            pltpu.SemaphoreType.DMA((2, 4)),
            pltpu.SemaphoreType.DMA((2,)),
        ],
        compiler_params=params(),
    )(where, mid, col_near, col_far, row_near)


def even_odd_order():
    perm = np.zeros((W, W), ml_dtypes.bfloat16)
    perm[np.arange(W), np.concatenate([np.arange(0, W, 2), np.arange(1, W, 2)])] = 1
    return jnp.asarray(np.stack([perm, perm.T]))


def pieces_of(x):
    out = []
    for _ in range(3):
        out.append(x.astype(bf16))
        x = x - out[-1].astype(f32)
    return out


def reordered(order, x):
    a, b, c = pieces_of(x)
    x = (dot(order[0], a) + dot(order[0], b)) + dot(order[0], c)
    a, b, c = pieces_of(x)
    return (dot(a, order[1]) + dot(b, order[1])) + dot(c, order[1])


PROBE = (4, 4, 4, 16, W)


def block_rows(x, y, c):
    return pl.ds(pl.multiple_of((x % 2) * 128 + y * 32 + c * 16, 16), 16)


def ext_pieces(where, ext, mid, row_near, row_far, col_near, col_far):
    rows, cols = rim_starts(where)
    inner = pl.ds(H, W)
    full = pl.ds(0, 2 * W)
    return [
        (mid, ext.at[:, :, inner, inner]),
        (row_near, ext.at[:, :, pl.ds(rows[0], H), inner]),
        (row_far, ext.at[:, :, pl.ds(rows[1], H), inner]),
        (col_near, ext.at[:, :, full, pl.ds(cols[0], H)]),
        (col_far, ext.at[:, :, full, pl.ds(cols[1], H)]),
    ]


def extract(pos, ext, win):
    lane = lax.broadcasted_iota(jnp.int32, (W + 8, H), 1)
    sub = lax.broadcasted_iota(jnp.int32, (W // 8, 8, H), 1)
    for s in range(SLOTS):
        rows, cols, dr, dc = corner(pos, s)
        for j in range(2):
            for p in range(2):
                turned = [pltpu.roll(ext[j, p, rows, col], (H - dc) % H, 1) for col in cols]
                for k in range(2):
                    x = jnp.where(lane < H - dc, turned[k], turned[k + 1])
                    x = pltpu.roll(x.reshape(W // 8 + 1, 8, H), (8 - dr) % 8, 1)
                    x = jnp.where(sub < 8 - dr, x[:-1], x[1:])
                    win[s, j, p, :, k * H : k * H + H] = x.reshape(W, H)


def place(pos, grad, ext, j):
    lane = lax.broadcasted_iota(jnp.int32, (W + 8, H), 1)
    sub = lax.broadcasted_iota(jnp.int32, (W // 8 + 1, 8, H), 1)
    group = jnp.zeros((1, 8, H), f32)
    ext[j] = jnp.zeros(ext.shape[1:], f32)
    for s in range(SLOTS):
        rows, cols, dr, dc = corner(pos, s)
        for p in range(2):
            turned = []
            for k in range(2):
                x = grad[s, j, p, :, k * H : k * H + H].reshape(W // 8, 8, H)
                x = pltpu.roll(x, dr, 1)
                x = jnp.where(
                    sub >= dr,
                    jnp.concatenate([x, group], 0),
                    jnp.concatenate([group, x], 0),
                )
                turned.append(pltpu.roll(x.reshape(W + 8, H), dc, 1))
            ext[j, p, rows, cols[0]] += jnp.where(lane >= dc, turned[0], 0.0)
            ext[j, p, rows, cols[1]] += jnp.where(lane >= dc, turned[1], turned[0])
            ext[j, p, rows, cols[2]] += jnp.where(lane >= dc, 0.0, turned[1])


def times(x, y):
    return x[0] * y[0] - x[1] * y[1], x[0] * y[1] + x[1] * y[0]


def times_conj(x, y):
    return x[0] * y[0] + x[1] * y[1], x[1] * y[0] - x[0] * y[1]


def read(ref, *index):
    return ref[(*index, 0)], ref[(*index, 1)]


def write(ref, value, *index):
    for part in range(2):
        ref[(*index, part)] = value[part]


def add_to(ref, value, *index):
    for part in range(2):
        at = (*index, part)
        ref[at] += value[part]


def forward_step(tabs, probe, win, u, far, intensity, m):
    slots = range(SLOTS)
    here = read(probe, m)
    fields = propagate(tabs, [times(here, read(win, s, 0)) for s in slots], False)
    for s in slots:
        write(u, fields[s], m, s)
    fields = dft(tabs, [times(fields[s], read(win, s, 1)) for s in slots])
    for s in slots:
        write(far, fields[s], m, s)
        power = fields[s][0] * fields[s][0] + fields[s][1] * fields[s][1]
        intensity[s] += power


def backward_step(tabs, probe, win, u, far, scale, grad_probe, grad_win, m, between):
    slots = range(SLOTS)
    fields = [tuple(scale[s] * part for part in read(far, m, s)) for s in slots]
    fields = dft_adjoint(tabs, fields)
    for s in slots:
        add_to(grad_win, times_conj(fields[s], read(u, m, s)), s, 1)
    between()
    fields = propagate(tabs, [times_conj(fields[s], read(win, s, 1)) for s in slots], True)
    here = read(probe, m)
    for s in slots:
        add_to(grad_win, times_conj(fields[s], here), s, 0)
    terms = [times_conj(fields[s], read(win, s, 0)) for s in slots]
    write(grad_probe, tuple(a + b for a, b in zip(*terms)))


def main_kernel(
    loss_scale, where, pos, counts, order, high, low, mine, other, meas, meas_core, meas_far, meas_far_core,
    mid, row_near, row_far, col_near, col_far,
    out_mine, out_other, out_mid, out_row_near, out_row_far, out_col_near, out_col_far,
    ext, win, probe, u, far, scale, grad_probe, grad_win, blocks, out_blocks, hi, lo, rows, pattern, perm,
    meas_sems, ext_sems, table_sems, probe_sems, out_sems,
):
    c, h, xl = where[0], where[1], where[2]
    pairs = [(meas.at[:, h, c], rows.at[0, 0]), (meas_core, rows.at[0, 1])]
    pairs += [(meas_far.at[:, c], rows.at[1, 0]), (meas_far_core, rows.at[1, 1]), (order, perm)]
    meas_copies = start_all(pairs, meas_sems)
    ext_copies = start_all(ext_pieces(where, ext, mid, row_near, row_far, col_near, col_far), ext_sems)
    table_copies = start_all([(high, hi), (low, lo)], table_sems)

    def probe_copies(m):
        pairs = ((mine, 0), (other, 1))
        return [pltpu.make_async_copy(a.at[m], blocks.at[k, m], probe_sems.at[m, k]) for a, k in pairs]

    for m in range(MODES):
        for copy in probe_copies(m):
            copy.start()
    scale[...] = jnp.zeros_like(scale)
    grad_win[...] = jnp.zeros_like(grad_win)
    wait_all(meas_copies)
    for s in range(SLOTS):
        for i, half in ((0, h), (1, 1 - h)):
            for k, core in ((0, c), (1, 1 - c)):
                for y in range(4):
                    start = pl.multiple_of(half * H + y * 32 + core * 16, 16)
                    pattern[s, pl.ds(start, 16), :] = rows[i, k, y, s]
        pattern[s] = reordered(perm, pattern[s])
    wait_all(ext_copies)
    extract(pos, ext, win)
    wait_all(table_copies)
    tabs = (hi, lo)

    def forward(m, _):
        wait_all(probe_copies(m))
        for k in range(4):
            x = (2 * xl + h + k) % 4
            for y in range(4):
                probe[m, x // 2, block_rows(x, y, c), :] = blocks[0, m, k, y]
                probe[m, x // 2, block_rows(x, y, 1 - c), :] = blocks[1, m, k, y]
        forward_step(tabs, probe, win, u, far, scale, m)
        return 0

    lax.fori_loop(0, MODES, forward, 0, unroll=2)
    for s in range(SLOTS):
        weight = jnp.where(s < counts[0, 0], 2.0 * loss_scale, 0.0)
        scale[s] = weight * (1.0 - pattern[s] * lax.rsqrt(scale[s] + amp_floor))

    def out_copies(m):
        pairs = ((out_mine, 0), (out_other, 1))
        return [pltpu.make_async_copy(out_blocks.at[k, m], a.at[m], probe_sems.at[m, k]) for a, k in pairs]

    def backward(m, between):
        backward_step(tabs, probe, win, u, far, scale, grad_probe, grad_win, m, between)
        for x in range(4):
            for y in range(4):
                out_blocks[0, m, y, x] = grad_probe[x // 2, block_rows(x, y, c), :]
                out_blocks[1, m, y, x] = grad_probe[x // 2, block_rows(x, y, 1 - c), :]
        for copy in out_copies(m):
            copy.start()
        return 0

    def place_slice(j):
        place(pos, grad_win, ext, j)
        pairs = ext_pieces(where, ext, out_mid, out_row_near, out_row_far, out_col_near, out_col_far)
        return start_all([(b.at[j], a.at[j]) for a, b in pairs], out_sems.at[j])

    copies = []
    lax.fori_loop(0, MODES - 1, lambda m, _: backward(m, lambda: None), 0, unroll=3)
    backward(MODES - 1, lambda: copies.extend(place_slice(1)))
    copies += place_slice(0)
    for m in range(MODES):
        copies += out_copies(m)
    wait_all(copies)


def gradients(tabs, loss_scale, where, pos, counts, *arrays):
    return pl.pallas_call(
        functools.partial(main_kernel, loss_scale),
        in_specs=[SMEM] * 3 + [HBM] * 14,
        out_specs=[HBM] * 7,
        out_shape=[
            struct(*PROBE),
            struct(*PROBE),
            struct(2, 2, W, W),
            struct(2, 2, H, W),
            struct(2, 2, H, W),
            struct(2, 2, 2 * W, H),
            struct(2, 2, 2 * W, H),
        ],
        scratch_shapes=[
            pltpu.VMEM((2, 2, 2 * W, 2 * W), f32),
            pltpu.VMEM((SLOTS, 2, 2, W, W), f32),
            pltpu.VMEM((MODES, 2, W, W), f32),
            pltpu.VMEM((MODES, SLOTS, 2, W, W), f32),
            pltpu.VMEM((MODES, SLOTS, 2, W, W), f32),
            pltpu.VMEM((SLOTS, W, W), f32),
            pltpu.VMEM((2, W, W), f32),
            pltpu.VMEM((SLOTS, 2, 2, W, W), f32),
            pltpu.VMEM((2,) + PROBE, f32),
            pltpu.VMEM((2,) + PROBE, f32),
            pltpu.VMEM((8, W, W), bf16),
            pltpu.VMEM((8, W, W), bf16),
            pltpu.VMEM((2, 2, 4, SLOTS, 16, W), f32),
            pltpu.VMEM((SLOTS, W, W), f32),
            pltpu.VMEM((2, W, W), bf16),
            pltpu.SemaphoreType.DMA((5,)),
            pltpu.SemaphoreType.DMA((5,)),
            pltpu.SemaphoreType.DMA((2,)),
            pltpu.SemaphoreType.DMA((MODES, 2)),
            pltpu.SemaphoreType.DMA((2, 5)),
        ],
        compiler_params=pltpu.CompilerParams(vmem_limit_bytes=MAIN_BYTES),
        cost_estimate=cost(32),
    )(where, pos, counts, even_odd_order(), *tabs, *arrays)


TY = ("z", "xl")
TX = ("xh", "y", "c")
PLANE = ("xl", "xh", "y")
SWAP = [(0, 1), (1, 0)]


def far_pairs(count):
    return [(i, i + 1) for i in range(1, count - 1, 2)] + [(i + 1, i) for i in range(1, count - 1, 2)]


def after(x, *earlier):
    return lax.optimization_barrier((x,) + earlier)[0]


def exchange(x, axes):
    return lax.all_to_all(x, axes, split_axis=0, concat_axis=0, tiled=True)


def pick(x, index, axis):
    return lax.dynamic_index_in_dim(x, index, axis, keepdims=False)


def swap_rows(near, far):
    return lax.ppermute(near, "xl", SWAP), lax.ppermute(far, TY, far_pairs(8))


def swap_columns(near, far):
    return lax.ppermute(near, "c", SWAP), lax.ppermute(far, TX, far_pairs(16))


def body(object_slices, probe_rows, measured, positions, counts):
    tabs = tuple(jnp.asarray(t) for t in make_tables())
    pos = positions[0, 0]
    where = jnp.stack([lax.axis_index(name) for name in ("c", "xh", "xl")])

    mid = object_slices
    near, far = row_slices(where, mid)
    row_near, row_far = swap_rows(near, far)
    tiles = measured.reshape(2, 4, 2, SLOTS, 16, W).transpose(1, 0, 2, 3, 4, 5).reshape(4, 128, W)
    spread = jnp.broadcast_to(probe_rows[None], (4, 16, W))
    both = exchange(jnp.concatenate([spread, tiles], 1), "y")
    probe_rows = both[:, :16].reshape(64, W)
    meas = both[:, 16:].reshape(4, 2, 2, SLOTS, 16, W)
    c, h = where[0], where[1]
    meas_far = lax.ppermute(pick(meas, 1 - h, 1), "xh", SWAP)
    meas_core = lax.ppermute(pick(pick(meas, h, 1), 1 - c, 1), "c", SWAP)
    meas_far_core = lax.ppermute(pick(meas_far, 1 - c, 1), "c", SWAP)
    probe_rows = [probe_rows] + [
        lax.ppermute(probe_rows, ("xl", "xh"), [((i + k) % 4, i) for i in range(4)]) for k in range(1, 4)
    ]
    probe_rows = after(jnp.stack(probe_rows), row_near, row_far)
    mine = exchange(jnp.broadcast_to(probe_rows.reshape(1, 256, W), (4, 256, W)), "z")
    mine = mine.reshape(*PROBE)
    near, far = column_slices(where, mid, row_near, row_far)
    col_near, col_far = swap_columns(near, far)
    other = lax.ppermute(after(mine, meas_far), "c", SWAP)
    mine, other, mid, row_near, row_far, col_near, col_far = gradients(
        tabs, 1.0 / 16.0, where, pos, counts, mine, other, meas, meas_core, meas_far, meas_far_core,
        mid, row_near, row_far, col_near, col_far,
    )
    mine = mine + lax.ppermute(other, "c", SWAP)
    col_near, col_far = swap_columns(col_near, col_far)
    mine = exchange(mine.reshape(4, 256, W), "z")
    near, far = rims(where, row_near, row_far, col_near, col_far)
    row_near, row_far = swap_rows(near, far)
    mine = jnp.sum(after(mine, near, far), 0).reshape(4, 4, 16, W)
    total = jnp.sum(exchange(mine, "y"), 0)
    x = 2 * where[2] + h
    parts = [
        lax.ppermute(pick(total, (x + k) % 4, 0), ("xl", "xh"), [(i, (i + k) % 4) for i in range(4)])
        for k in range(1, 4)
    ]
    probe_grad = pick(total, x, 0) + parts[0] + parts[1] + parts[2]
    mid = after(mid, mine)
    held = combine_near(where, mid, col_near, col_far, row_near)
    corner_at = (0, 0, where[2] * H, 0)
    far = lax.dynamic_slice(held, corner_at, (2, 2, H, W)) + row_far
    return lax.dynamic_update_slice(held, far, corner_at), probe_grad


def solution(mesh):
    fine = Mesh(mesh.devices.reshape(4, 2, 2, 4, 2), ("z", "xl", "xh", "y", "c"))
    in_specs = (
        P(None, None, TY, TX),
        P(TY + TX, None),
        P(TY, None, None, TX, None),
        P(TY, TX, None, None),
        P(TY, TX),
    )
    out_specs = (P(None, None, TY, TX), P(TY + TX, None))
    return jax.shard_map(
        body, mesh=fine, in_specs=in_specs, out_specs=out_specs, check_vma=False
    )
```
